32 devices in a mesh: chan: 8 (over z, y), win: 4 (over x, core).
Axes of the slice: x: 2, y: 2, z: 4, core: 2. Of those that a mesh axis runs over, the one named last changes fastest.
Arguments:
- strain: float32 [8, 64, 4096], P('win', 'chan'), may hold values from -6 to 6
- offset_limit: int32 [64], P('chan'), may hold values from 32 to 256
- alive: int32 [64], P('chan'), may hold values 0 or 1
Outputs:
- stacked: float32 [256, 64, 400], P('win', 'chan')
The draws below stay inside these ranges and needn't reach their ends.
All inputs are finite; a program needn't handle non-finite values. No bound on the sum of `alive` on one device may be relied on, other than what follows from the above.
Results may differ from the reference program's by a relative error of at most 0.0003.
Values sent between devices are 32-bit elements; how exact they have to be, the bound alone decides.
No kernel may reach another device: no remote copies, remote signals or barrier semaphores. Data moves between devices by JAX's collectives and lax.ppermute only.
A program may use at most 64 MiB of HBM per device.

```python
import math
import jax
import jax.numpy as jnp
from jax import lax

SAMPLES = 4096
NF = 256
MAXOFF = 256
MAXLAG = 200
CHANNELS = 64
WINDOWS = 8


def with_ends(entries, own_key, smallest, largest):
    dims = entries.shape
    spot = [jax.random.randint(jax.random.fold_in(own_key, axis), (), 0, dims[axis]) for axis in range(len(dims))]
    entries = entries.at[tuple(spot)].set(smallest)
    longest = dims.index(max(dims))
    spot[longest] = (spot[longest] + 1) % dims[longest]
    return entries.at[tuple(spot)].set(largest)


def steps_of(key, shape, split, least, top_value):
    gain = 1.0
    for axis_at, blocks in split:
        draws = jax.random.uniform(jax.random.fold_in(jax.random.fold_in(key, 6), axis_at), (blocks,), jnp.float32, least / len(split), top_value / len(split))
        gain = gain * jnp.repeat(jnp.exp(draws), shape[axis_at] // blocks).reshape((-1,) + (1,) * (len(shape) - 1 - axis_at))
    return gain


def centred(key, extent, deviation, bound, pieces=(), kind=jnp.bfloat16):
    entries = jax.random.normal(key, extent, jnp.float32) * deviation
    if len(pieces) > 0:
        entries = steps_of(key, extent, pieces, -0.22, 0.18) * entries
    return jnp.clip(entries, min=-bound, max=bound).astype(kind)


def setup_inputs(seed: int = 0) -> dict:
    arg_keys = jax.random.split(jax.random.key(seed), 4)
    strain = centred(arg_keys[0], (WINDOWS, CHANNELS, SAMPLES), 1.0, 6.0, ((0, 4), (1, 8)), jnp.float32)
    offset_limit = with_ends(jax.random.randint(arg_keys[1], (CHANNELS,), MAXOFF // 8, MAXOFF + 1), jax.random.fold_in(arg_keys[1], 1), MAXOFF // 8, MAXOFF).astype(jnp.int32)
    alive = with_ends((jax.random.randint(arg_keys[2], (CHANNELS,), 0, 16) < 15).astype(jnp.int32), jax.random.fold_in(arg_keys[2], 1), 0, 1)
    return {"strain": strain, "offset_limit": offset_limit, "alive": alive}


EPS = 1e-06
WHITEN_BINS = 64

def forward_table(first, count, length, nbins):
    sample_ids = first + jnp.arange(count, dtype=jnp.int32)
    freq_ids = jnp.arange(1, nbins + 1, dtype=jnp.int32)
    phases = sample_ids[:, None] * freq_ids[None, :] % length
    angles = phases.astype(jnp.float32) * (2.0 * math.pi / length)
    return jnp.concatenate([jnp.cos(angles), -jnp.sin(angles)], axis=1)

def inverse_table(nbins, half_lags, length):
    freq_ids = jnp.arange(1, nbins + 1, dtype=jnp.int32)
    lag_ids = jnp.arange(-half_lags, half_lags, dtype=jnp.int32)
    phases = freq_ids[:, None] * lag_ids[None, :] % length
    angles = phases.astype(jnp.float32) * (2.0 * math.pi / length)
    return jnp.concatenate([jnp.cos(angles), -jnp.sin(angles)], axis=0)

def whiten(spectrum):
    nbins = spectrum.shape[-1] // 2
    real_part = spectrum[..., :nbins]
    imag_part = spectrum[..., nbins:]
    magnitude = jnp.sqrt(real_part * real_part + imag_part * imag_part)
    blocked = magnitude.reshape(magnitude.shape[:-1] + (nbins // WHITEN_BINS, WHITEN_BINS))
    levels = lax.optimization_barrier(jnp.mean(blocked, axis=-1, keepdims=True)) + EPS
    levels = jnp.broadcast_to(levels, blocked.shape).reshape(magnitude.shape)
    return spectrum / jnp.concatenate([levels, levels], axis=-1)

def cross_pair(own_rows, partner):
    nbins = own_rows.shape[-1] // 2
    own_re = own_rows[..., None, :nbins]
    own_im = own_rows[..., None, nbins:]
    part_re = partner[..., :nbins]
    part_im = partner[..., nbins:]
    real_sum = lax.optimization_barrier(jnp.sum(own_re * part_re + own_im * part_im, axis=0))
    imag_sum = lax.optimization_barrier(jnp.sum(own_im * part_re - own_re * part_im, axis=0))
    return jnp.concatenate([real_sum, imag_sum], axis=-1)

def reference(strain, offset_limit, alive):
    windows, channels, samples = strain.shape
    table = forward_table(0, samples, samples, NF)
    spectrum = jnp.dot(strain.reshape(windows * channels, samples), table, precision=lax.Precision.HIGHEST, preferred_element_type=jnp.float32)
    white = whiten(spectrum.reshape(windows, channels, 2 * NF))
    white = white * alive.astype(jnp.float32)[None, :, None]
    padded = jnp.concatenate([white, jnp.zeros((windows, MAXOFF, 2 * NF), jnp.float32)], axis=1)
    inverse = inverse_table(NF, MAXLAG, samples)
    scale = 1.0 / math.sqrt(NF * windows)
    group = math.gcd(channels, 16)
    offset_ids = jnp.arange(1, MAXOFF + 1, dtype=jnp.int32)

    def one_group(first):
        row_ids = first + jnp.arange(group, dtype=jnp.int32)
        index_table = (row_ids[:, None] + offset_ids[None, :]).astype(jnp.int32)
        own_rows = lax.dynamic_slice_in_dim(white, first, group, 1)
        partner = jnp.take(padded, index_table.reshape(-1), axis=1).reshape(windows, group, MAXOFF, 2 * NF)
        cross = cross_pair(own_rows, partner)
        limits = lax.dynamic_slice_in_dim(offset_limit, first, group, 0)
        keep = (offset_ids[None, :] <= limits[:, None]).astype(jnp.float32)
        cross = cross * keep[:, :, None]
        lagged = jnp.dot(cross.reshape(group * MAXOFF, 2 * NF), inverse, precision=lax.Precision.HIGHEST, preferred_element_type=jnp.float32)
        return (lagged * scale).reshape(group, MAXOFF, 2 * MAXLAG)
    starts = jnp.arange(0, channels, group, dtype=jnp.int32)
    result = lax.map(one_group, starts)
    return result.reshape(channels, MAXOFF, 2 * MAXLAG).transpose(1, 0, 2)
```

```python
import functools
import math

import jax
import jax.numpy as jnp
import ml_dtypes
import numpy as np
from jax import lax
from jax.experimental import pallas as pl
from jax.experimental.pallas import tpu as pltpu
from jax.sharding import PartitionSpec as P

NF = 256
MAXOFF = 256
MAXLAG = 200
EPS = 1e-06
WHITEN_BINS = 64
LANES = 128
SUB = 8
TILES = 2 * NF // LANES
BF16 = jnp.bfloat16
F32 = jnp.float32
MIB = 1 << 20


def split(table):
    high = table.astype(ml_dtypes.bfloat16)
    low = (table - high.astype(np.float64)).astype(ml_dtypes.bfloat16)
    return high, low


def phase(product, length):
    return (product % length) * (2.0 * math.pi / length)


def forward_tables(samples, chunk):
    freq = np.arange(1, NF + 1, dtype=np.int64)
    inner = phase(np.arange(chunk, dtype=np.int64)[:, None] * freq[None, :], samples)
    outer = phase(np.arange(samples // chunk, dtype=np.int64)[:, None] * chunk * freq[None, :], samples)
    twiddle = np.concatenate([np.cos(outer), np.sin(outer)], axis=1).astype(np.float32)
    return split(np.concatenate([np.cos(inner), -np.sin(inner)], axis=1)) + (twiddle,)


def inverse_tables(samples, scale):
    freq = np.arange(1, NF + 1, dtype=np.int64)
    lags = np.arange(-MAXLAG, MAXLAG, dtype=np.int64)
    angles = phase(freq[:, None] * lags[None, :], samples)
    return split(scale * np.concatenate([np.cos(angles), -np.sin(angles)], axis=0))


def halves(value):
    high = value.astype(BF16)
    return high, (value - high.astype(F32)).astype(BF16)


def mm(a, b):
    return jnp.dot(a, b, preferred_element_type=F32)


def column(ref, count):
    rows = lax.broadcasted_iota(jnp.int32, (count, LANES), 0)
    value = jnp.zeros((count, LANES), jnp.int32)
    for index in range(count):
        value = jnp.where(rows == index, ref[index], value)
    return value


def whiten_kernel(alive_ref, strain_ref, high_ref, low_ref, twiddle_ref, white_ref):
    wins, chans, samples = strain_ref.shape
    rows = wins * chans
    chunk = high_ref.shape[0]
    strain = strain_ref[...].reshape(rows, samples)
    pieces = samples // chunk
    stacked = jnp.concatenate([strain[:, a * chunk : (a + 1) * chunk] for a in range(pieces)], axis=0)
    x_high, x_low = halves(stacked)
    part = mm(x_high, high_ref[...]) + mm(x_high, low_ref[...]) + mm(x_low, high_ref[...])
    real = jnp.zeros((rows, NF), F32)
    imag = jnp.zeros((rows, NF), F32)
    for a in range(pieces):
        p_re = part[a * rows : (a + 1) * rows, :NF]
        p_im = part[a * rows : (a + 1) * rows, NF:]
        cos = twiddle_ref[a : a + 1, :NF]
        sin = twiddle_ref[a : a + 1, NF:]
        real = real + p_re * cos + p_im * sin
        imag = imag + p_im * cos - p_re * sin
    magnitude = jnp.sqrt(real * real + imag * imag)
    block_r = lax.broadcasted_iota(jnp.int32, (NF, NF), 0) // WHITEN_BINS
    block_c = lax.broadcasted_iota(jnp.int32, (NF, NF), 1) // WHITEN_BINS
    mean = jnp.where(block_r == block_c, 1.0 / WHITEN_BINS, 0.0).astype(BF16)
    m_high, m_low = halves(magnitude)
    level = mm(m_high, mean) + mm(m_low, mean) + EPS
    live = column(alive_ref, chans).astype(F32)
    for w in range(wins):
        keep = slice(w * chans, (w + 1) * chans)
        for tile in range(TILES):
            source = real if tile < TILES // 2 else imag
            lanes = slice(tile % (TILES // 2) * LANES, (tile % (TILES // 2) + 1) * LANES)
            white_ref[(tile * wins + w) * chans : (tile * wins + w + 1) * chans, :] = (
                source[keep, lanes] / level[keep, lanes] * live
            )


def whiten(strain, alive):
    wins, chans, samples = strain.shape
    chunk = min(256, samples)
    high, low, twiddle = forward_tables(samples, chunk)
    rows = wins * chans
    return pl.pallas_call(
        whiten_kernel,
        out_shape=jax.ShapeDtypeStruct((TILES * rows, LANES), F32),
        in_specs=[pl.BlockSpec(memory_space=pltpu.SMEM)] + [pl.BlockSpec(memory_space=pltpu.VMEM)] * 4,
        out_specs=pl.BlockSpec(memory_space=pltpu.VMEM),
        compiler_params=pltpu.CompilerParams(vmem_limit_bytes=32 * MIB),
        cost_estimate=pl.CostEstimate(flops=6 * rows * samples * 2 * NF, bytes_accessed=4 * rows * samples, transcendentals=0),
        name="whiten",
    )(alive, strain, high, low, twiddle)


def correlate_kernel(orders, wins, chans, share, lead_only, limit_ref, *refs):
    count = len(orders)
    blocks = refs[:count]
    high_ref, low_ref, out_ref = refs[count : count + 3]
    own, partner, x_high, x_low, lagged, in_sem, out_sem = refs[count + 3 :]
    groups = own.shape[0]
    octets = share // SUB
    place = lax.axis_index("win")

    def load(index):
        copies = []
        for position in range(groups):
            group = orders[index][position]
            target = own.at[group] if index == 0 else partner.at[group, :, :, pl.ds((index - 1) * chans, chans), :]
            copies.append(pltpu.make_async_copy(blocks[index].at[position], target, in_sem.at[index, position]))
        return copies

    def store(first, rows, source):
        return pltpu.make_async_copy(source, out_ref.at[pl.ds(first, rows)], out_sem.at[first // SUB])

    def work():
        copies = [copy for index in range(count) for copy in load(index)]
        for copy in copies:
            copy.start()
        limit = column(limit_ref, chans)
        have = (count - 1) * chans
        total = partner.shape[3]
        if have < total:
            partner[:, :, :, have:, :] = jnp.zeros(partner.shape[:3] + (total - have, LANES), F32)
        for copy in copies:
            copy.wait()
        row_ids = lax.broadcasted_iota(jnp.int32, (chans, LANES), 0)
        half = TILES // 2

        def octet(g, carry):
            first = pl.multiple_of(g * SUB, SUB)
            sums = [[jnp.zeros((chans, LANES), F32) for _ in range(TILES)] for _ in range(SUB)]
            for group in range(groups):
                for w in range(wins):
                    mine = [own[group, t, w] for t in range(TILES)]
                    now = [partner[group, t, w, pl.ds(first, SUB), :] for t in range(TILES)]
                    later = [partner[group, t, w, pl.ds(first + SUB, SUB), :] for t in range(TILES)]
                    for j in range(SUB):
                        if j + 1 < SUB:
                            theirs = [
                                pltpu.roll(jnp.where(row_ids > j, now[t], later[t]), SUB - 1 - j, 0)
                                for t in range(TILES)
                            ]
                        else:
                            theirs = later
                        for t in range(half):
                            a_re, a_im, b_re, b_im = mine[t], mine[t + half], theirs[t], theirs[t + half]
                            sums[j][t] = sums[j][t] + (a_re * b_re + a_im * b_im)
                            sums[j][t + half] = sums[j][t + half] + (a_im * b_re - a_re * b_im)
            offset = place * share + first
            for j in range(0, SUB, 2):
                pair = []
                for k in (j, j + 1):
                    keep = limit > offset + k
                    pair.append(jnp.concatenate([jnp.where(keep, value, 0.0) for value in sums[k]], axis=1))
                high, low = halves(jnp.concatenate(pair, axis=0))
                rows = pl.ds(pl.multiple_of((first + j) * chans, 2 * chans), 2 * chans)
                x_high[rows, :] = high
                x_low[rows, :] = low
            return carry

        step = octets // 2
        stores = []
        for part in range(2):
            lax.fori_loop(part * step, (part + 1) * step, octet, 0)
            rows = slice(part * step * SUB * chans, (part + 1) * step * SUB * chans)
            result = (
                mm(x_high[rows, :], high_ref[...]) + mm(x_high[rows, :], low_ref[...]) + mm(x_low[rows, :], high_ref[...])
            )
            lagged[part * step * SUB : (part + 1) * step * SUB] = result.reshape(step * SUB, chans, result.shape[1])
            copy = store(part * step * SUB, step * SUB, lagged.at[pl.ds(part * step * SUB, step * SUB)])
            copy.start()
            stores.append(copy)
        for copy in stores:
            copy.wait()

    def blank():
        step = octets // 2 * SUB
        lagged[:step] = jnp.zeros((step,) + lagged.shape[1:], F32)
        stores = [store(part * step, step, lagged.at[pl.ds(0, step)]) for part in range(2)]
        for copy in stores:
            copy.start()
        for copy in stores:
            copy.wait()

    if lead_only:
        pl.when(place == 0)(work)
        pl.when(place != 0)(blank)
    else:
        work()


def correlate(blocks, orders, offset_limit, wins, chans, share, samples, scale, lead_only):
    high, low = inverse_tables(samples, scale)
    groups = len(orders[0])
    shape = (groups, TILES, wins, chans, LANES)
    octets = share // SUB
    rows = share * chans
    lags = 2 * MAXLAG
    body = functools.partial(correlate_kernel, orders, wins, chans, share, lead_only)
    return pl.pallas_call(
        body,
        out_shape=jax.ShapeDtypeStruct((share, chans, lags), F32),
        in_specs=[pl.BlockSpec(memory_space=pltpu.SMEM)]
        + [pl.BlockSpec(memory_space=pl.ANY)] * len(blocks)
        + [pl.BlockSpec(memory_space=pltpu.VMEM)] * 2,
        out_specs=pl.BlockSpec(memory_space=pl.ANY),
        scratch_shapes=[
            pltpu.VMEM(shape, F32),
            pltpu.VMEM((groups, TILES, wins, share + SUB, LANES), F32),
            pltpu.VMEM((rows, 2 * NF), BF16),
            pltpu.VMEM((rows, 2 * NF), BF16),
            pltpu.VMEM((share, chans, lags), F32),
            pltpu.SemaphoreType.DMA((len(blocks), groups)),
            pltpu.SemaphoreType.DMA((octets,)),
        ],
        compiler_params=pltpu.CompilerParams(vmem_limit_bytes=32 * MIB),
        cost_estimate=pl.CostEstimate(flops=6 * rows * 2 * NF * lags, bytes_accessed=4 * rows * lags, transcendentals=0),
        name="correlate",
    )(offset_limit, *[block.reshape(shape) for block in blocks], high, low)


def local(strain, offset_limit, alive):
    win_dev, ch_dev, samples = strain.shape
    win_count = lax.axis_size("win")
    chan_count = lax.axis_size("chan")
    scale = 1.0 / math.sqrt(NF * win_dev * win_count)
    share = MAXOFF // win_count
    reach = share // ch_dev
    axes = ("chan", "win")
    finish = functools.partial(
        correlate,
        offset_limit=offset_limit,
        wins=win_dev,
        chans=ch_dev,
        share=share,
        samples=samples,
        scale=scale,
    )
    white = whiten(strain, alive)

    def device(chan, win):
        return chan * win_count + win

    def exchange(value, mask):
        pairs = [(device(c, w), device(c, w ^ mask)) for c in range(chan_count) for w in range(win_count)]
        return lax.ppermute(value, axes, pairs)

    def ahead(steps, source, target):
        return [(device(c + steps, source), device(c, target)) for c in range(chan_count - steps)]

    if win_count == 4 and chan_count * ch_dev <= share:
        block = white
        for mask in (2, 1):
            block = jnp.concatenate([block, exchange(block, mask)], axis=0)
        relative = (0, 2, 1, 3)
        near = (chan_count + 1) // 2
        blocks = [block, block]
        orders = [relative, relative]
        far, far_orders = [], []
        for k in range(chan_count - near):
            pairs = ahead(near + k, 3, 1)
            if k + 1 < near:
                pairs = pairs + ahead(k + 1, 0, 0)
            got = lax.ppermute(block, axes, pairs)
            if k + 1 < near:
                blocks.append(got)
                orders.append(relative)
            far.append(exchange(got, 1))
            far_orders.append(tuple(3 ^ r for r in relative))
        return finish(blocks + far, orders + far_orders, lead_only=True)

    gathered = lax.all_gather(white, "win", tiled=True)
    order = tuple(range(win_count))
    blocks = [gathered]
    for steps in range(reach + 1):
        pairs = [
            (device(c + reach * w + steps, w), device(c, w))
            for w in range(win_count)
            for c in range(chan_count)
            if c + reach * w + steps < chan_count
        ]
        blocks.append(lax.ppermute(gathered, axes, pairs) if pairs else jnp.zeros_like(gathered))
    return finish(blocks, [order] * len(blocks), lead_only=False)


def solution(mesh):
    in_specs = (P("win", "chan", None), P("chan"), P("chan"))
    out_specs = P("win", "chan", None)
    return jax.shard_map(local, mesh=mesh, in_specs=in_specs, out_specs=out_specs, check_vma=False)
```

```python
import functools
import math

import jax
import jax.numpy as jnp
import ml_dtypes
import numpy as np
from jax import lax
from jax.experimental import pallas as pl
from jax.experimental.pallas import tpu as pltpu
from jax.sharding import PartitionSpec as P

NF = 256
MAXOFF = 256
MAXLAG = 200
EPS = 1e-06
WHITEN_BINS = 64
LANES = 128
SUB = 8
TILES = 2 * NF // LANES
BF16 = jnp.bfloat16
F32 = jnp.float32
MIB = 1 << 20


def split(table):
    high = table.astype(ml_dtypes.bfloat16)
    low = (table - high.astype(np.float64)).astype(ml_dtypes.bfloat16)
    return high, low


def phase(product, length):
    return (product % length) * (2.0 * math.pi / length)


def forward_tables(samples, chunk):
    freq = np.arange(1, NF + 1, dtype=np.int64)
    inner = phase(np.arange(chunk, dtype=np.int64)[:, None] * freq[None, :], samples)
    outer = phase(np.arange(samples // chunk, dtype=np.int64)[:, None] * chunk * freq[None, :], samples)
    twiddle = np.concatenate([np.cos(outer), np.sin(outer)], axis=1).astype(np.float32)
    return split(np.concatenate([np.cos(inner), -np.sin(inner)], axis=1)) + (twiddle,)


def inverse_tables(samples, scale):
    freq = np.arange(1, NF + 1, dtype=np.int64)
    lags = np.arange(-MAXLAG, MAXLAG, dtype=np.int64)
    angles = phase(freq[:, None] * lags[None, :], samples)
    return split(scale * np.concatenate([np.cos(angles), -np.sin(angles)], axis=0))


def halves(value):
    high = value.astype(BF16)
    return high, (value - high.astype(F32)).astype(BF16)


def mm(a, b):
    return jnp.dot(a, b, preferred_element_type=F32)


def column(ref, count):
    rows = lax.broadcasted_iota(jnp.int32, (count, LANES), 0)
    value = jnp.zeros((count, LANES), jnp.int32)
    for index in range(count):
        value = jnp.where(rows == index, ref[index], value)
    return value


def whiten_kernel(alive_hbm, limit_hbm, strain_hbm, table_hbm, twiddle_hbm, white_ref, limit_out, *scratch):
    alive_ref, limit_ref, strain_ref, table_ref, twiddle_ref, sems = scratch
    wins, chans, samples = strain_ref.shape
    chunk = table_ref.shape[0] // 2
    copies = [
        pltpu.make_async_copy(source, target, sems.at[index])
        for index, (source, target) in enumerate(
            [
                (strain_hbm, strain_ref),
                (table_hbm, table_ref),
                (twiddle_hbm, twiddle_ref),
                (alive_hbm, alive_ref),
                (limit_hbm, limit_ref),
            ]
        )
    ]
    for copy in copies:
        copy.start()
    for copy in copies:
        copy.wait()
    rows = wins * chans
    strain = strain_ref[...].reshape(rows, samples)
    pieces = samples // chunk
    stacked = jnp.concatenate([strain[:, a * chunk : (a + 1) * chunk] for a in range(pieces)], axis=0)
    x_high, x_low = halves(stacked)
    high = table_ref[:chunk, :]
    part = mm(x_high, high) + mm(x_high, table_ref[chunk:, :]) + mm(x_low, high)
    real = jnp.zeros((rows, NF), F32)
    imag = jnp.zeros((rows, NF), F32)
    for a in range(pieces):
        p_re = part[a * rows : (a + 1) * rows, :NF]
        p_im = part[a * rows : (a + 1) * rows, NF:]
        cos = twiddle_ref[a : a + 1, :NF]
        sin = twiddle_ref[a : a + 1, NF:]
        real = real + p_re * cos + p_im * sin
        imag = imag + p_im * cos - p_re * sin
    magnitude = jnp.sqrt(real * real + imag * imag)
    block_r = lax.broadcasted_iota(jnp.int32, (NF, NF), 0) // WHITEN_BINS
    block_c = lax.broadcasted_iota(jnp.int32, (NF, NF), 1) // WHITEN_BINS
    mean = jnp.where(block_r == block_c, 1.0 / WHITEN_BINS, 0.0).astype(BF16)
    m_high, m_low = halves(magnitude)
    level = mm(m_high, mean) + mm(m_low, mean) + EPS
    live = column(alive_ref, chans).astype(F32)
    limit_out[...] = column(limit_ref, chans)
    for w in range(wins):
        keep = slice(w * chans, (w + 1) * chans)
        for tile in range(TILES):
            source = real if tile < TILES // 2 else imag
            lanes = slice(tile % (TILES // 2) * LANES, (tile % (TILES // 2) + 1) * LANES)
            white_ref[(tile * wins + w) * chans : (tile * wins + w + 1) * chans, :] = (
                source[keep, lanes] / level[keep, lanes] * live
            )


def whiten(strain, alive, offset_limit):
    wins, chans, samples = strain.shape
    chunk = min(256, samples)
    high, low, twiddle = forward_tables(samples, chunk)
    table = np.concatenate([high, low], axis=0)
    rows = wins * chans
    return pl.pallas_call(
        whiten_kernel,
        out_shape=(
            jax.ShapeDtypeStruct((TILES * rows, LANES), F32),
            jax.ShapeDtypeStruct((chans, LANES), jnp.int32),
        ),
        in_specs=[pl.BlockSpec(memory_space=pltpu.HBM)] * 5,
        out_specs=(pl.BlockSpec(memory_space=pltpu.VMEM),) * 2,
        scratch_shapes=[
            pltpu.SMEM((chans,), jnp.int32),
            pltpu.SMEM((chans,), jnp.int32),
            pltpu.VMEM(strain.shape, F32),
            pltpu.VMEM(table.shape, BF16),
            pltpu.VMEM(twiddle.shape, F32),
            pltpu.SemaphoreType.DMA((5,)),
        ],
        compiler_params=pltpu.CompilerParams(vmem_limit_bytes=32 * MIB),
        cost_estimate=pl.CostEstimate(flops=6 * rows * samples * 2 * NF, bytes_accessed=4 * rows * samples, transcendentals=0),
        name="whiten",
    )(*[pltpu.with_memory_space_constraint(jnp.asarray(x), pltpu.HBM) for x in (alive, offset_limit, strain, table, twiddle)])


def correlate_kernel(orders, wins, chans, share, lead_only, limit_ref, *refs):
    count = len(orders)
    blocks = refs[:count]
    high_ref, low_ref, out_ref = refs[count : count + 3]
    own, partner, x_high, x_low, lagged, in_sem, out_sem = refs[count + 3 :]
    groups = own.shape[0]
    octets = share // SUB
    place = lax.axis_index("win")

    def load(index):
        copies = []
        for position in range(groups):
            group = orders[index][position]
            target = own.at[group] if index == 0 else partner.at[group, :, :, pl.ds((index - 1) * chans, chans), :]
            copies.append(pltpu.make_async_copy(blocks[index].at[position], target, in_sem.at[index, position]))
        return copies

    def store(first, rows, source):
        return pltpu.make_async_copy(source, out_ref.at[pl.ds(first, rows)], out_sem.at[first // SUB])

    def work():
        copies = [copy for index in range(count) for copy in load(index)]
        for copy in copies:
            copy.start()
        limit = limit_ref[...]
        have = (count - 1) * chans
        total = partner.shape[3]
        if have < total:
            partner[:, :, :, have:, :] = jnp.zeros(partner.shape[:3] + (total - have, LANES), F32)
        for copy in copies:
            copy.wait()
        half = TILES // 2

        def octet(g, carry):
            first = pl.multiple_of(g * SUB, SUB)
            sums = [[jnp.zeros((chans, LANES), F32) for _ in range(TILES)] for _ in range(SUB)]
            for group in range(groups):
                for w in range(wins):
                    mine = [own[group, t, w] for t in range(TILES)]
                    for j in range(SUB):
                        theirs = [partner[group, t, w, pl.ds(first + j + 1, SUB), :] for t in range(TILES)]
                        for t in range(half):
                            a_re, a_im, b_re, b_im = mine[t], mine[t + half], theirs[t], theirs[t + half]
                            sums[j][t] = sums[j][t] + (a_re * b_re + a_im * b_im)
                            sums[j][t + half] = sums[j][t + half] + (a_im * b_re - a_re * b_im)
            offset = place * share + first
            for j in range(0, SUB, 2):
                pair = []
                for k in (j, j + 1):
                    keep = limit > offset + k
                    pair.append(jnp.concatenate([jnp.where(keep, value, 0.0) for value in sums[k]], axis=1))
                high, low = halves(jnp.concatenate(pair, axis=0))
                rows = pl.ds(pl.multiple_of((first + j) * chans, 2 * chans), 2 * chans)
                x_high[rows, :] = high
                x_low[rows, :] = low
            return carry

        step = octets // 2
        stores = []
        for part in range(2):
            lax.fori_loop(part * step, (part + 1) * step, octet, 0)
            rows = slice(part * step * SUB * chans, (part + 1) * step * SUB * chans)
            result = (
                mm(x_high[rows, :], high_ref[...]) + mm(x_high[rows, :], low_ref[...]) + mm(x_low[rows, :], high_ref[...])
            )
            lagged[part * step * SUB : (part + 1) * step * SUB] = result.reshape(step * SUB, chans, result.shape[1])
            copy = store(part * step * SUB, step * SUB, lagged.at[pl.ds(part * step * SUB, step * SUB)])
            copy.start()
            stores.append(copy)
        for copy in stores:
            copy.wait()

    def blank():
        step = octets // 2 * SUB
        lagged[:step] = jnp.zeros((step,) + lagged.shape[1:], F32)
        stores = [store(part * step, step, lagged.at[pl.ds(0, step)]) for part in range(2)]
        for copy in stores:
            copy.start()
        for copy in stores:
            copy.wait()

    if lead_only:
        pl.when(place == 0)(work)
        pl.when(place != 0)(blank)
    else:
        work()


def correlate(blocks, orders, limit, wins, chans, share, samples, scale, lead_only):
    high, low = inverse_tables(samples, scale)
    groups = len(orders[0])
    shape = (groups, TILES, wins, chans, LANES)
    octets = share // SUB
    rows = share * chans
    lags = 2 * MAXLAG
    body = functools.partial(correlate_kernel, orders, wins, chans, share, lead_only)
    return pl.pallas_call(
        body,
        out_shape=jax.ShapeDtypeStruct((share, chans, lags), F32),
        in_specs=[pl.BlockSpec(memory_space=pltpu.VMEM)]
        + [pl.BlockSpec(memory_space=pl.ANY)] * len(blocks)
        + [pl.BlockSpec(memory_space=pltpu.VMEM)] * 2,
        out_specs=pl.BlockSpec(memory_space=pl.ANY),
        scratch_shapes=[
            pltpu.VMEM(shape, F32),
            pltpu.VMEM((groups, TILES, wins, share + SUB, LANES), F32),
            pltpu.VMEM((rows, 2 * NF), BF16),
            pltpu.VMEM((rows, 2 * NF), BF16),
            pltpu.VMEM((share, chans, lags), F32),
            pltpu.SemaphoreType.DMA((len(blocks), groups)),
            pltpu.SemaphoreType.DMA((octets,)),
        ],
        compiler_params=pltpu.CompilerParams(vmem_limit_bytes=32 * MIB),
        cost_estimate=pl.CostEstimate(flops=6 * rows * 2 * NF * lags, bytes_accessed=4 * rows * lags, transcendentals=0),
        name="correlate",
    )(limit, *[block.reshape(shape) for block in blocks], high, low)


def local(strain, offset_limit, alive):
    win_dev, ch_dev, samples = strain.shape
    win_count = lax.axis_size("win")
    chan_count = lax.axis_size("chan")
    scale = 1.0 / math.sqrt(NF * win_dev * win_count)
    share = MAXOFF // win_count
    reach = share // ch_dev
    axes = ("chan", "win")
    white, limit = whiten(strain, alive, offset_limit)
    finish = functools.partial(
        correlate,
        limit=limit,
        wins=win_dev,
        chans=ch_dev,
        share=share,
        samples=samples,
        scale=scale,
    )

    def device(chan, win):
        return chan * win_count + win

    def exchange(value, mask):
        pairs = [(device(c, w), device(c, w ^ mask)) for c in range(chan_count) for w in range(win_count)]
        return lax.ppermute(value, axes, pairs)

    def ahead(steps, source, target):
        return [(device(c + steps, source), device(c, target)) for c in range(chan_count - steps)]

    if win_count == 4 and chan_count * ch_dev <= share:
        block = white
        for mask in (2, 1):
            block = jnp.concatenate([block, exchange(block, mask)], axis=0)
        relative = (0, 2, 1, 3)
        crossed = tuple(3 ^ r for r in relative)
        blocks, orders = {0: block}, {0: relative}
        blocks[1], orders[1] = lax.ppermute(block, axes, ahead(1, 0, 0)), relative
        for even in range(2, chan_count, 2):
            pairs = ahead(even, 3, 0) + ahead(even + 1, 0, 1)
            blocks[even], orders[even] = lax.ppermute(block, axes, pairs), crossed
            if even + 1 < chan_count:
                blocks[even + 1], orders[even + 1] = exchange(blocks[even], 1), relative
        near = range(chan_count)
        return finish([block] + [blocks[d] for d in near], [relative] + [orders[d] for d in near], lead_only=True)

    gathered = lax.all_gather(white, "win", tiled=True)
    order = tuple(range(win_count))
    blocks = [gathered]
    for steps in range(reach + 1):
        pairs = [
            (device(c + reach * w + steps, w), device(c, w))
            for w in range(win_count)
            for c in range(chan_count)
            if c + reach * w + steps < chan_count
        ]
        blocks.append(lax.ppermute(gathered, axes, pairs) if pairs else jnp.zeros_like(gathered))
    return finish(blocks, [order] * len(blocks), lead_only=False)


def solution(mesh):
    in_specs = (P("win", "chan", None), P("chan"), P("chan"))
    out_specs = P("win", "chan", None)
    return jax.shard_map(local, mesh=mesh, in_specs=in_specs, out_specs=out_specs, check_vma=False)
```

```python
import functools
import itertools
import math

import jax
import jax.numpy as jnp
import ml_dtypes
import numpy as np
from jax import lax
from jax.experimental import pallas as pl
from jax.experimental.pallas import tpu as pltpu
from jax.sharding import PartitionSpec as P

NF = 256
MAXOFF = 256
MAXLAG = 200
EPS = 1e-06
WHITEN_BINS = 64
LANES = 128
SUB = 8
TILES = 2 * NF // LANES
BF16 = jnp.bfloat16
F32 = jnp.float32
MIB = 1 << 20


def split(table):
    high = table.astype(ml_dtypes.bfloat16)
    low = (table - high.astype(np.float64)).astype(ml_dtypes.bfloat16)
    return high, low


def phase(product, length):
    return (product % length) * (2.0 * math.pi / length)


def forward_tables(samples, chunk):
    freq = np.arange(1, NF + 1, dtype=np.int64)
    inner = phase(np.arange(chunk, dtype=np.int64)[:, None] * freq[None, :], samples)
    outer = phase(np.arange(samples // chunk, dtype=np.int64)[:, None] * chunk * freq[None, :], samples)
    twiddle = np.concatenate([np.cos(outer), np.sin(outer)], axis=1).astype(np.float32)
    return split(np.concatenate([np.cos(inner), -np.sin(inner)], axis=1)) + (twiddle,)


def inverse_tables(samples, scale):
    freq = np.arange(1, NF + 1, dtype=np.int64)
    lags = np.arange(-MAXLAG, MAXLAG, dtype=np.int64)
    angles = phase(freq[:, None] * lags[None, :], samples)
    return split(scale * np.concatenate([np.cos(angles), -np.sin(angles)], axis=0))


def halves(value):
    high = value.astype(BF16)
    return high, (value - high.astype(F32)).astype(BF16)


def mm(a, b):
    return jnp.dot(a, b, preferred_element_type=F32)


def column(ref, count):
    rows = lax.broadcasted_iota(jnp.int32, (count, LANES), 0)
    value = jnp.zeros((count, LANES), jnp.int32)
    for index in range(count):
        value = jnp.where(rows == index, ref[index], value)
    return value


def whiten_kernel(alive_hbm, limit_hbm, strain_hbm, table_hbm, twiddle_hbm, white_ref, limit_out, *scratch):
    alive_ref, limit_ref, strain_ref, table_ref, twiddle_ref, sems = scratch
    wins, chans, samples = strain_ref.shape
    chunk = table_ref.shape[0] // 2
    copies = [
        pltpu.make_async_copy(source, target, sems.at[index])
        for index, (source, target) in enumerate(
            [
                (strain_hbm, strain_ref),
                (table_hbm, table_ref),
                (twiddle_hbm, twiddle_ref),
                (alive_hbm, alive_ref),
                (limit_hbm, limit_ref),
            ]
        )
    ]
    for copy in copies:
        copy.start()
    for copy in copies:
        copy.wait()
    rows = wins * chans
    strain = strain_ref[...].reshape(rows, samples)
    pieces = samples // chunk
    stacked = jnp.concatenate([strain[:, a * chunk : (a + 1) * chunk] for a in range(pieces)], axis=0)
    x_high, x_low = halves(stacked)
    high = table_ref[:chunk, :]
    part = mm(x_high, high) + mm(x_high, table_ref[chunk:, :]) + mm(x_low, high)
    real = jnp.zeros((rows, NF), F32)
    imag = jnp.zeros((rows, NF), F32)
    for a in range(pieces):
        p_re = part[a * rows : (a + 1) * rows, :NF]
        p_im = part[a * rows : (a + 1) * rows, NF:]
        cos = twiddle_ref[a : a + 1, :NF]
        sin = twiddle_ref[a : a + 1, NF:]
        real = real + p_re * cos + p_im * sin
        imag = imag + p_im * cos - p_re * sin
    magnitude = jnp.sqrt(real * real + imag * imag)
    block_r = lax.broadcasted_iota(jnp.int32, (NF, NF), 0) // WHITEN_BINS
    block_c = lax.broadcasted_iota(jnp.int32, (NF, NF), 1) // WHITEN_BINS
    mean = jnp.where(block_r == block_c, 1.0 / WHITEN_BINS, 0.0).astype(BF16)
    m_high, m_low = halves(magnitude)
    level = mm(m_high, mean) + mm(m_low, mean) + EPS
    live = column(alive_ref, chans).astype(F32)
    limit_out[...] = column(limit_ref, chans)
    for w in range(wins):
        keep = slice(w * chans, (w + 1) * chans)
        for tile in range(TILES):
            source = real if tile < TILES // 2 else imag
            lanes = slice(tile % (TILES // 2) * LANES, (tile % (TILES // 2) + 1) * LANES)
            white_ref[(tile * wins + w) * chans : (tile * wins + w + 1) * chans, :] = (
                source[keep, lanes] / level[keep, lanes] * live
            )


def whiten(strain, alive, offset_limit):
    wins, chans, samples = strain.shape
    chunk = min(256, samples)
    high, low, twiddle = forward_tables(samples, chunk)
    table = np.concatenate([high, low], axis=0)
    rows = wins * chans
    return pl.pallas_call(
        whiten_kernel,
        out_shape=(
            jax.ShapeDtypeStruct((TILES * rows, LANES), F32),
            jax.ShapeDtypeStruct((chans, LANES), jnp.int32),
        ),
        in_specs=[pl.BlockSpec(memory_space=pltpu.HBM)] * 5,
        out_specs=(pl.BlockSpec(memory_space=pltpu.VMEM),) * 2,
        scratch_shapes=[
            pltpu.SMEM((chans,), jnp.int32),
            pltpu.SMEM((chans,), jnp.int32),
            pltpu.VMEM(strain.shape, F32),
            pltpu.VMEM(table.shape, BF16),
            pltpu.VMEM(twiddle.shape, F32),
            pltpu.SemaphoreType.DMA((5,)),
        ],
        compiler_params=pltpu.CompilerParams(vmem_limit_bytes=32 * MIB),
        cost_estimate=pl.CostEstimate(flops=6 * rows * samples * 2 * NF, bytes_accessed=4 * rows * samples, transcendentals=0),
        name="whiten",
    )(*[pltpu.with_memory_space_constraint(jnp.asarray(x), pltpu.HBM) for x in (alive, offset_limit, strain, table, twiddle)])


def correlate_kernel(orders, ahead, wins, chans, share, octets, has_tail, *refs):
    count = len(orders)
    limit_ref = refs[0]
    blocks = refs[1 : count + 1]
    high_ref, low_ref = refs[count + 1 : count + 3]
    rest = refs[count + 3 :]
    tail_ref = rest[0] if has_tail else None
    out_ref, own, partner, x_high, x_low, lagged, in_sem, out_sem = rest[has_tail:]
    groups = own.shape[0]
    first_octet, last_octet = octets
    size = (last_octet - first_octet) * SUB
    place = lax.axis_index("win")

    def load(index):
        copies = []
        for position in range(groups):
            group = orders[index][position]
            target = own.at[group] if index == 0 else partner.at[group, :, :, pl.ds((index - 1) * chans, chans), :]
            copies.append(pltpu.make_async_copy(blocks[index].at[position], target, in_sem.at[index, position]))
        return copies

    def store(source, first, rows, which):
        return pltpu.make_async_copy(source, out_ref.at[pl.ds(first, rows)], out_sem.at[which])

    def work():
        copies = [load(index) for index in range(count)]
        for group in copies:
            for copy in group:
                copy.start()
        stores = []
        if has_tail:
            stores.append(store(tail_ref, size, tail_ref.shape[0], octets[1]))
            stores[0].start()
        limit = limit_ref[...]
        have = (count - 1) * chans
        total = partner.shape[3]
        if have < total:
            partner[:, :, :, have:, :] = jnp.zeros(partner.shape[:3] + (total - have, LANES), F32)
        for index, group in enumerate(copies):
            for copy in group:
                copy.wait()
            if ahead is not None and index > 0 and ahead[index - 1] > 0:

                def clear(first=(index - 1) * chans):
                    partner[:, :, :, first : first + chans, :] = jnp.zeros(partner.shape[:3] + (chans, LANES), F32)

                pl.when(lax.axis_index("chan") + ahead[index - 1] >= lax.axis_size("chan"))(clear)
        half = TILES // 2

        def octet(g):
            first = g * SUB
            sums = [[jnp.zeros((chans, LANES), F32) for _ in range(TILES)] for _ in range(SUB)]
            for group in range(groups):
                for w in range(wins):
                    mine = [own[group, t, w] for t in range(TILES)]
                    for j in range(SUB):
                        theirs = [partner[group, t, w, pl.ds(first + j + 1, SUB), :] for t in range(TILES)]
                        for t in range(half):
                            a_re, a_im, b_re, b_im = mine[t], mine[t + half], theirs[t], theirs[t + half]
                            sums[j][t] = sums[j][t] + (a_re * b_re + a_im * b_im)
                            sums[j][t + half] = sums[j][t + half] + (a_im * b_re - a_re * b_im)
            offset = place * share + first_octet * SUB + first
            for j in range(0, SUB, 2):
                pair = []
                for k in (j, j + 1):
                    keep = limit > offset + k
                    pair.append(jnp.concatenate([jnp.where(keep, value, 0.0) for value in sums[k]], axis=1))
                high, low = halves(jnp.concatenate(pair, axis=0))
                rows = slice((first + j) * chans, (first + j + 2) * chans)
                x_high[rows, :] = high
                x_low[rows, :] = low

        step = math.gcd(last_octet - first_octet, 4)
        for part in range(0, last_octet - first_octet, step):
            for g in range(part, part + step):
                octet(g)
            rows = slice(part * SUB * chans, (part + step) * SUB * chans)
            result = (
                mm(x_high[rows, :], high_ref[...]) + mm(x_high[rows, :], low_ref[...]) + mm(x_low[rows, :], high_ref[...])
            )
            lagged[part * SUB : (part + step) * SUB] = result.reshape(step * SUB, chans, result.shape[1])
            copy = store(lagged.at[pl.ds(part * SUB, step * SUB)], part * SUB, step * SUB, part)
            copy.start()
            stores.append(copy)
        for copy in stores:
            copy.wait()

    def blank():
        lagged[...] = jnp.zeros(lagged.shape, F32)
        stores = [store(lagged, 0, size, 0)]
        if has_tail:
            stores.append(store(tail_ref, size, tail_ref.shape[0], octets[1]))
        for copy in stores:
            copy.start()
        for copy in stores:
            copy.wait()

    if ahead is None:
        work()
    else:
        pl.when(place == 0)(work)
        pl.when(place != 0)(blank)


def correlate(blocks, orders, ahead, octets, tail, limit, wins, chans, share, samples, scale):
    high, low = inverse_tables(samples, scale)
    groups = len(orders[0])
    shape = (groups, TILES, wins, chans, LANES)
    size = (octets[1] - octets[0]) * SUB
    rows = size * chans
    lags = 2 * MAXLAG
    tails = [] if tail is None else [tail]
    body = functools.partial(correlate_kernel, orders, ahead, wins, chans, share, octets, len(tails))
    whole = size + sum(t.shape[0] for t in tails)
    return pl.pallas_call(
        body,
        out_shape=jax.ShapeDtypeStruct((whole, chans, lags), F32),
        in_specs=[pl.BlockSpec(memory_space=pltpu.VMEM)]
        + [pl.BlockSpec(memory_space=pl.ANY)] * len(blocks)
        + [pl.BlockSpec(memory_space=pltpu.VMEM)] * 2
        + [pl.BlockSpec(memory_space=pl.ANY)] * len(tails),
        out_specs=pl.BlockSpec(memory_space=pl.ANY),
        scratch_shapes=[
            pltpu.VMEM(shape, F32),
            pltpu.VMEM((groups, TILES, wins, size + SUB, LANES), F32),
            pltpu.VMEM((rows, 2 * NF), BF16),
            pltpu.VMEM((rows, 2 * NF), BF16),
            pltpu.VMEM((size, chans, lags), F32),
            pltpu.SemaphoreType.DMA((len(blocks), groups)),
            pltpu.SemaphoreType.DMA((share // SUB + 1,)),
        ],
        compiler_params=pltpu.CompilerParams(vmem_limit_bytes=32 * MIB),
        cost_estimate=pl.CostEstimate(flops=6 * rows * 2 * NF * lags, bytes_accessed=4 * rows * lags, transcendentals=0),
        name="correlate",
    )(limit, *[block.reshape(shape) for block in blocks], high, low, *tails)


def local(strain, offset_limit, alive):
    win_dev, ch_dev, samples = strain.shape
    win_count = lax.axis_size("win")
    chan_count = lax.axis_size("chan")
    scale = 1.0 / math.sqrt(NF * win_dev * win_count)
    share = MAXOFF // win_count
    reach = share // ch_dev
    axes = ("chan", "win")
    white, limit = whiten(strain, alive, offset_limit)
    finish = functools.partial(
        correlate,
        limit=limit,
        wins=win_dev,
        chans=ch_dev,
        share=share,
        samples=samples,
        scale=scale,
    )

    def device(chan, win):
        return chan * win_count + win

    def exchange(value, mask):
        pairs = [(device(c, w), device(c, w ^ mask)) for c in range(chan_count) for w in range(win_count)]
        return lax.ppermute(value, axes, pairs)

    def shift(wanted):
        sources = [w for w in range(win_count) if w not in [source for _, source in wanted.values()]]
        targets = [w for w in range(win_count) if w not in wanted]

        def cost(order):
            return sum(100 if s == t else (s ^ t) // 2 for s, t in zip(order, targets))

        idle = dict(zip(targets, min(itertools.permutations(sources), key=cost)))
        moves = {**wanted, **{target: (0, source) for target, source in idle.items()}}
        return [
            (device((c + steps) % chan_count, source), device(c, target))
            for target, (steps, source) in moves.items()
            for c in range(chan_count)
        ]

    if win_count == 4 and chan_count * ch_dev <= share:
        block = white
        for mask in (2, 1):
            block = jnp.concatenate([block, exchange(block, mask)], axis=0)
        relative = (0, 2, 1, 3)
        flip = lambda source: tuple(source ^ r for r in relative)
        blocks, orders = {0: block}, {0: relative}
        for even in range(2, chan_count, 2):
            wanted = {0: (even, 3)}
            if even + 1 < chan_count:
                wanted[1] = (even + 1, 1)
            blocks[even], orders[even] = lax.ppermute(block, axes, shift(wanted)), flip(3)
            if even + 1 < chan_count:
                blocks[even + 1], orders[even + 1] = exchange(blocks[even], 1), flip(1)
        if chan_count > 1:
            blocks[1], orders[1] = lax.ppermute(block, axes, shift({0: (1, 1)})), flip(1)

        def part(octets, tail):
            near = [d for d in range(octets[0], octets[1] + 1) if d < chan_count]
            return finish(
                [block] + [blocks[d] for d in near],
                [relative] + [orders[d] for d in near],
                near,
                octets,
                tail,
            )

        cut = min(4, reach)
        return part((0, cut), part((cut, reach), None) if cut < reach else None)

    gathered = lax.all_gather(white, "win", tiled=True)
    order = tuple(range(win_count))
    blocks = [gathered]
    for steps in range(reach + 1):
        pairs = [
            (device(c + reach * w + steps, w), device(c, w))
            for w in range(win_count)
            for c in range(chan_count)
            if c + reach * w + steps < chan_count
        ]
        blocks.append(lax.ppermute(gathered, axes, pairs) if pairs else jnp.zeros_like(gathered))
    return finish(blocks, [order] * len(blocks), None, (0, reach), None)


def solution(mesh):
    in_specs = (P("win", "chan", None), P("chan"), P("chan"))
    out_specs = P("win", "chan", None)
    return jax.shard_map(local, mesh=mesh, in_specs=in_specs, out_specs=out_specs, check_vma=False)
```

```python
import functools
import itertools
import math

import jax
import jax.numpy as jnp
import ml_dtypes
import numpy as np
from jax import lax
from jax.experimental import pallas as pl
from jax.experimental.pallas import tpu as pltpu
from jax.sharding import PartitionSpec as P

NF = 256
MAXOFF = 256
MAXLAG = 200
EPS = 1e-06
WHITEN_BINS = 64
LANES = 128
SUB = 8
TILES = 2 * NF // LANES
BF16 = jnp.bfloat16
F32 = jnp.float32
MIB = 1 << 20


def split(table):
    high = table.astype(ml_dtypes.bfloat16)
    low = (table - high.astype(np.float64)).astype(ml_dtypes.bfloat16)
    return high, low


def phase(product, length):
    return (product % length) * (2.0 * math.pi / length)


def forward_tables(samples, chunk):
    freq = np.arange(1, NF + 1, dtype=np.int64)
    inner = phase(np.arange(chunk, dtype=np.int64)[:, None] * freq[None, :], samples)
    outer = phase(np.arange(samples // chunk, dtype=np.int64)[:, None] * chunk * freq[None, :], samples)
    twiddle = np.concatenate([np.cos(outer), np.sin(outer)], axis=1).astype(np.float32)
    return split(np.concatenate([np.cos(inner), -np.sin(inner)], axis=1)) + (twiddle,)


def inverse_tables(samples, scale):
    freq = np.arange(1, NF + 1, dtype=np.int64)
    lags = np.arange(-MAXLAG, MAXLAG, dtype=np.int64)
    angles = phase(freq[:, None] * lags[None, :], samples)
    return split(scale * np.concatenate([np.cos(angles), -np.sin(angles)], axis=0))


def halves(value):
    high = value.astype(BF16)
    return high, (value - high.astype(F32)).astype(BF16)


def mm(a, b):
    return jnp.dot(a, b, preferred_element_type=F32)


def column(ref, count):
    rows = lax.broadcasted_iota(jnp.int32, (count, LANES), 0)
    value = jnp.zeros((count, LANES), jnp.int32)
    for index in range(count):
        value = jnp.where(rows == index, ref[index], value)
    return value


def whiten_kernel(alive_hbm, limit_hbm, strain_hbm, table_hbm, twiddle_hbm, white_ref, limit_out, *scratch):
    alive_ref, limit_ref, strain_ref, table_ref, twiddle_ref, sems = scratch
    wins, chans, samples = strain_ref.shape
    chunk = table_ref.shape[0] // 2
    copies = [
        pltpu.make_async_copy(source, target, sems.at[index])
        for index, (source, target) in enumerate(
            [
                (strain_hbm, strain_ref),
                (table_hbm, table_ref),
                (twiddle_hbm, twiddle_ref),
                (alive_hbm, alive_ref),
                (limit_hbm, limit_ref),
            ]
        )
    ]
    for copy in copies:
        copy.start()
    for copy in copies:
        copy.wait()
    rows = wins * chans
    strain = strain_ref[...].reshape(rows, samples)
    pieces = samples // chunk
    stacked = jnp.concatenate([strain[:, a * chunk : (a + 1) * chunk] for a in range(pieces)], axis=0)
    x_high, x_low = halves(stacked)
    high = table_ref[:chunk, :]
    part = mm(x_high, high) + mm(x_high, table_ref[chunk:, :]) + mm(x_low, high)
    real = jnp.zeros((rows, NF), F32)
    imag = jnp.zeros((rows, NF), F32)
    for a in range(pieces):
        p_re = part[a * rows : (a + 1) * rows, :NF]
        p_im = part[a * rows : (a + 1) * rows, NF:]
        cos = twiddle_ref[a : a + 1, :NF]
        sin = twiddle_ref[a : a + 1, NF:]
        real = real + p_re * cos + p_im * sin
        imag = imag + p_im * cos - p_re * sin
    magnitude = jnp.sqrt(real * real + imag * imag)
    block_r = lax.broadcasted_iota(jnp.int32, (NF, NF), 0) // WHITEN_BINS
    block_c = lax.broadcasted_iota(jnp.int32, (NF, NF), 1) // WHITEN_BINS
    mean = jnp.where(block_r == block_c, 1.0 / WHITEN_BINS, 0.0).astype(BF16)
    m_high, m_low = halves(magnitude)
    level = mm(m_high, mean) + mm(m_low, mean) + EPS
    live = column(alive_ref, chans).astype(F32)
    limit_out[...] = column(limit_ref, chans)
    for w in range(wins):
        keep = slice(w * chans, (w + 1) * chans)
        for tile in range(TILES):
            source = real if tile < TILES // 2 else imag
            lanes = slice(tile % (TILES // 2) * LANES, (tile % (TILES // 2) + 1) * LANES)
            white_ref[(tile * wins + w) * chans : (tile * wins + w + 1) * chans, :] = (
                source[keep, lanes] / level[keep, lanes] * live
            )


def whiten(strain, alive, offset_limit):
    wins, chans, samples = strain.shape
    chunk = min(256, samples)
    high, low, twiddle = forward_tables(samples, chunk)
    table = np.concatenate([high, low], axis=0)
    rows = wins * chans
    return pl.pallas_call(
        whiten_kernel,
        out_shape=(
            jax.ShapeDtypeStruct((TILES * rows, LANES), F32),
            jax.ShapeDtypeStruct((chans, LANES), jnp.int32),
        ),
        in_specs=[pl.BlockSpec(memory_space=pltpu.HBM)] * 5,
        out_specs=(pl.BlockSpec(memory_space=pltpu.VMEM),) * 2,
        scratch_shapes=[
            pltpu.SMEM((chans,), jnp.int32),
            pltpu.SMEM((chans,), jnp.int32),
            pltpu.VMEM(strain.shape, F32),
            pltpu.VMEM(table.shape, BF16),
            pltpu.VMEM(twiddle.shape, F32),
            pltpu.SemaphoreType.DMA((5,)),
        ],
        compiler_params=pltpu.CompilerParams(vmem_limit_bytes=32 * MIB),
        cost_estimate=pl.CostEstimate(flops=6 * rows * samples * 2 * NF, bytes_accessed=4 * rows * samples, transcendentals=0),
        name="whiten",
    )(*[pltpu.with_memory_space_constraint(jnp.asarray(x), pltpu.HBM) for x in (alive, offset_limit, strain, table, twiddle)])


def runs(octets):
    found = []
    for index, octet in enumerate(octets):
        if found and found[-1][1] + found[-1][2] == octet:
            found[-1][2] += 1
        else:
            found.append([index, octet, 1])
    return found


def correlate_kernel(orders, needed, octets, early, wins, chans, share, lead, *refs):
    count = len(orders)
    limit_ref = refs[0]
    blocks = refs[1 : count + 1]
    high_ref, low_ref = refs[count + 1 : count + 3]
    rest = refs[count + 3 :]
    early_ref = rest[0] if early else None
    out_ref, partner, x_high, x_low, lagged, out_sem, early_sem = rest[1 if early else 0 :]
    groups = partner.shape[0]
    place = lax.axis_index("win")

    def out_rows(first, length):
        return out_ref.at[pl.ds(first * SUB, length * SUB)]

    def early_stores():
        return [
            pltpu.make_async_copy(early_ref.at[pl.ds(at * SUB, length * SUB)], out_rows(octet, length), early_sem.at[at])
            for at, octet, length in runs(early)
        ]

    def stores():
        places = runs(octets) if early else [(0, 0, len(octets))]
        return [
            pltpu.make_async_copy(lagged.at[pl.ds(at * SUB, length * SUB)], out_rows(octet, length), out_sem.at[at])
            for at, octet, length in places
        ]

    def work():
        for copy in early_stores():
            copy.start()
        limit = limit_ref[...]
        chan, chan_count = lax.axis_index("chan"), lax.axis_size("chan")
        for index, steps in enumerate(needed):
            rows = slice(index * chans, (index + 1) * chans)
            if index + 1 >= count:
                partner[:, :, :, rows, :] = jnp.zeros(partner.shape[:3] + (chans, LANES), F32)
                continue
            for position in range(groups):
                value = blocks[index + 1][position]
                if lead and steps > 0:
                    value = jnp.where(chan + steps < chan_count, value, 0.0)
                partner[orders[index + 1][position], :, :, rows, :] = value
        own = {orders[0][position]: blocks[0].at[position] for position in range(groups)}
        half = TILES // 2
        for at, octet in enumerate(octets):
            first = needed.index(octet) * SUB
            sums = [[jnp.zeros((chans, LANES), F32) for _ in range(TILES)] for _ in range(SUB)]
            for group in range(groups):
                for w in range(wins):
                    mine = [own[group][t, w] for t in range(TILES)]
                    for j in range(SUB):
                        theirs = [partner[group, t, w, pl.ds(first + j + 1, SUB), :] for t in range(TILES)]
                        for t in range(half):
                            a_re, a_im, b_re, b_im = mine[t], mine[t + half], theirs[t], theirs[t + half]
                            sums[j][t] = sums[j][t] + (a_re * b_re + a_im * b_im)
                            sums[j][t + half] = sums[j][t + half] + (a_im * b_re - a_re * b_im)
            offset = place * share + octet * SUB
            for j in range(0, SUB, 2):
                pair = []
                for k in (j, j + 1):
                    keep = limit > offset + k
                    pair.append(jnp.concatenate([jnp.where(keep, value, 0.0) for value in sums[k]], axis=1))
                high, low = halves(jnp.concatenate(pair, axis=0))
                rows = slice((at * SUB + j) * chans, (at * SUB + j + 2) * chans)
                x_high[rows, :] = high
                x_low[rows, :] = low
        result = mm(x_high[...], high_ref[...]) + mm(x_high[...], low_ref[...]) + mm(x_low[...], high_ref[...])
        lagged[...] = result.reshape(lagged.shape)
        for copy in stores():
            copy.start()
        for copy in early_stores() + stores():
            copy.wait()

    def blank():
        lagged[...] = jnp.zeros(lagged.shape, F32)
        for copy in early_stores() + stores():
            copy.start()
        for copy in early_stores() + stores():
            copy.wait()

    if lead:
        pl.when(place == 0)(work)
        pl.when(place != 0)(blank)
    else:
        work()


def correlate(own, partners, octets, early, limit, wins, chans, share, samples, scale, lead):
    high, low = inverse_tables(samples, scale)
    needed = sorted({octet + step for octet in octets for step in (0, 1)})
    given = [own] + [partners[d] for d in needed if d in partners]
    orders = tuple(order for _, order in given)
    groups = len(orders[0])
    shape = (groups, TILES, wins, chans, LANES)
    size = len(octets) * SUB
    rows = size * chans
    lags = 2 * MAXLAG
    early_octets, early_result = early if early else ((), None)
    body = functools.partial(correlate_kernel, orders, needed, octets, early_octets, wins, chans, share, lead)
    return pl.pallas_call(
        body,
        out_shape=jax.ShapeDtypeStruct((size + len(early_octets) * SUB, chans, lags), F32),
        in_specs=[pl.BlockSpec(memory_space=pltpu.VMEM)]
        + [pl.BlockSpec(memory_space=pltpu.VMEM)] * len(given)
        + [pl.BlockSpec(memory_space=pltpu.VMEM)] * 2
        + [pl.BlockSpec(memory_space=pl.ANY)] * bool(early),
        out_specs=pl.BlockSpec(memory_space=pl.ANY),
        scratch_shapes=[
            pltpu.VMEM((groups, TILES, wins, len(needed) * SUB, LANES), F32),
            pltpu.VMEM((rows, 2 * NF), BF16),
            pltpu.VMEM((rows, 2 * NF), BF16),
            pltpu.VMEM((size, chans, lags), F32),
            pltpu.SemaphoreType.DMA((len(octets),)),
            pltpu.SemaphoreType.DMA((max(1, len(early_octets)),)),
        ],
        compiler_params=pltpu.CompilerParams(vmem_limit_bytes=32 * MIB),
        cost_estimate=pl.CostEstimate(flops=6 * rows * 2 * NF * lags, bytes_accessed=4 * rows * lags, transcendentals=0),
        name="correlate",
    )(limit, *[block.reshape(shape) for block, _ in given], high, low, *([early_result] if early else []))


def local(strain, offset_limit, alive):
    win_dev, ch_dev, samples = strain.shape
    win_count = lax.axis_size("win")
    chan_count = lax.axis_size("chan")
    scale = 1.0 / math.sqrt(NF * win_dev * win_count)
    share = MAXOFF // win_count
    reach = share // ch_dev
    axes = ("chan", "win")
    white, limit = whiten(strain, alive, offset_limit)
    finish = functools.partial(
        correlate,
        limit=limit,
        wins=win_dev,
        chans=ch_dev,
        share=share,
        samples=samples,
        scale=scale,
    )

    def device(chan, win):
        return chan * win_count + win

    def exchange(value, mask):
        pairs = [(device(c, w), device(c, w ^ mask)) for c in range(chan_count) for w in range(win_count)]
        return lax.ppermute(value, axes, pairs)

    def shift(wanted):
        sources = [w for w in range(win_count) if w not in [source for _, source in wanted.values()]]
        targets = [w for w in range(win_count) if w not in wanted]

        def cost(order):
            return sum(100 if s == t else (s ^ t) // 2 for s, t in zip(order, targets))

        idle = dict(zip(targets, min(itertools.permutations(sources), key=cost)))
        moves = {**wanted, **{target: (0, source) for target, source in idle.items()}}
        return [
            (device((c + steps) % chan_count, source), device(c, target))
            for target, (steps, source) in moves.items()
            for c in range(chan_count)
        ]

    if win_count == 4 and chan_count * ch_dev <= share:
        block = white
        for mask in (2, 1):
            block = jnp.concatenate([block, exchange(block, mask)], axis=0)

        def order(source):
            return tuple(source ^ r for r in (0, 2, 1, 3))

        partners = {0: (block, order(0))}
        for even in range(2, chan_count, 2):
            wanted = {0: (even, 3)}
            if even + 1 < chan_count:
                wanted[1] = (even + 1, 1)
            got = lax.ppermute(block, axes, shift(wanted))
            partners[even] = got, order(3)
            if even + 1 < chan_count:
                partners[even + 1] = exchange(got, 1), order(1)
        if chan_count > 1:
            partners[1] = lax.ppermute(block, axes, shift({0: (1, 1)})), order(1)
        return finish(partners[0], partners, list(range(reach)), None, lead=True)

    gathered = lax.all_gather(white, "win", tiled=True)
    order = tuple(range(win_count))
    partners = {}
    for steps in range(reach + 1):
        pairs = [
            (device(c + reach * w + steps, w), device(c, w))
            for w in range(win_count)
            for c in range(chan_count)
            if c + reach * w + steps < chan_count
        ]
        if pairs:
            partners[steps] = lax.ppermute(gathered, axes, pairs), order
    return finish((gathered, order), partners, list(range(reach)), None, lead=False)


def solution(mesh):
    in_specs = (P("win", "chan", None), P("chan"), P("chan"))
    out_specs = P("win", "chan", None)
    return jax.shard_map(local, mesh=mesh, in_specs=in_specs, out_specs=out_specs, check_vma=False)
```

```python
import functools
import itertools
import math

import jax
import jax.numpy as jnp
import ml_dtypes
import numpy as np
from jax import lax
from jax.experimental import pallas as pl
from jax.experimental.pallas import tpu as pltpu
from jax.sharding import PartitionSpec as P

NF = 256
MAXOFF = 256
MAXLAG = 200
EPS = 1e-06
WHITEN_BINS = 64
LANES = 128
SUB = 8
TILES = 2 * NF // LANES
BF16 = jnp.bfloat16
F32 = jnp.float32
MIB = 1 << 20


def split(table):
    high = table.astype(ml_dtypes.bfloat16)
    low = (table - high.astype(np.float64)).astype(ml_dtypes.bfloat16)
    return high, low


def phase(product, length):
    return (product % length) * (2.0 * math.pi / length)


def forward_tables(samples, chunk):
    freq = np.arange(1, NF + 1, dtype=np.int64)
    inner = phase(np.arange(chunk, dtype=np.int64)[:, None] * freq[None, :], samples)
    outer = phase(np.arange(samples // chunk, dtype=np.int64)[:, None] * chunk * freq[None, :], samples)
    twiddle = np.concatenate([np.cos(outer), np.sin(outer)], axis=1).astype(np.float32)
    return split(np.concatenate([np.cos(inner), -np.sin(inner)], axis=1)) + (twiddle,)


def inverse_tables(samples, scale):
    freq = np.arange(1, NF + 1, dtype=np.int64)
    lags = np.arange(-MAXLAG, MAXLAG, dtype=np.int64)
    angles = phase(freq[:, None] * lags[None, :], samples)
    return split(scale * np.concatenate([np.cos(angles), -np.sin(angles)], axis=0))


def halves(value):
    high = value.astype(BF16)
    return high, (value - high.astype(F32)).astype(BF16)


def mm(a, b):
    return jnp.dot(a, b, preferred_element_type=F32)


def column(ref, count):
    rows = lax.broadcasted_iota(jnp.int32, (count, LANES), 0)
    value = jnp.zeros((count, LANES), jnp.int32)
    for index in range(count):
        value = jnp.where(rows == index, ref[index], value)
    return value


def whiten_kernel(alive_hbm, limit_hbm, strain_hbm, table_hbm, twiddle_hbm, white_ref, limit_out, *scratch):
    alive_ref, limit_ref, strain_ref, table_ref, twiddle_ref, sems = scratch
    wins, chans, samples = strain_ref.shape
    chunk = table_ref.shape[0] // 2
    copies = [
        pltpu.make_async_copy(source, target, sems.at[index])
        for index, (source, target) in enumerate(
            [
                (strain_hbm, strain_ref),
                (table_hbm, table_ref),
                (twiddle_hbm, twiddle_ref),
                (alive_hbm, alive_ref),
                (limit_hbm, limit_ref),
            ]
        )
    ]
    for copy in copies:
        copy.start()
    for copy in copies:
        copy.wait()
    rows = wins * chans
    strain = strain_ref[...].reshape(rows, samples)
    pieces = samples // chunk
    stacked = jnp.concatenate([strain[:, a * chunk : (a + 1) * chunk] for a in range(pieces)], axis=0)
    x_high, x_low = halves(stacked)
    high = table_ref[:chunk, :]
    part = mm(x_high, high) + mm(x_high, table_ref[chunk:, :]) + mm(x_low, high)
    real = jnp.zeros((rows, NF), F32)
    imag = jnp.zeros((rows, NF), F32)
    for a in range(pieces):
        p_re = part[a * rows : (a + 1) * rows, :NF]
        p_im = part[a * rows : (a + 1) * rows, NF:]
        cos = twiddle_ref[a : a + 1, :NF]
        sin = twiddle_ref[a : a + 1, NF:]
        real = real + p_re * cos + p_im * sin
        imag = imag + p_im * cos - p_re * sin
    magnitude = jnp.sqrt(real * real + imag * imag)
    block_r = lax.broadcasted_iota(jnp.int32, (NF, NF), 0) // WHITEN_BINS
    block_c = lax.broadcasted_iota(jnp.int32, (NF, NF), 1) // WHITEN_BINS
    mean = jnp.where(block_r == block_c, 1.0 / WHITEN_BINS, 0.0).astype(BF16)
    m_high, m_low = halves(magnitude)
    level = mm(m_high, mean) + mm(m_low, mean) + EPS
    live = column(alive_ref, chans).astype(F32)
    limit_out[...] = column(limit_ref, chans)
    for w in range(wins):
        keep = slice(w * chans, (w + 1) * chans)
        for tile in range(TILES):
            source = real if tile < TILES // 2 else imag
            lanes = slice(tile % (TILES // 2) * LANES, (tile % (TILES // 2) + 1) * LANES)
            white_ref[(tile * wins + w) * chans : (tile * wins + w + 1) * chans, :] = (
                source[keep, lanes] / level[keep, lanes] * live
            )


def whiten(strain, alive, offset_limit):
    wins, chans, samples = strain.shape
    chunk = min(256, samples)
    high, low, twiddle = forward_tables(samples, chunk)
    table = np.concatenate([high, low], axis=0)
    rows = wins * chans
    return pl.pallas_call(
        whiten_kernel,
        out_shape=(
            jax.ShapeDtypeStruct((TILES * rows, LANES), F32),
            jax.ShapeDtypeStruct((chans, LANES), jnp.int32),
        ),
        in_specs=[pl.BlockSpec(memory_space=pltpu.HBM)] * 5,
        out_specs=(pl.BlockSpec(memory_space=pltpu.VMEM),) * 2,
        scratch_shapes=[
            pltpu.SMEM((chans,), jnp.int32),
            pltpu.SMEM((chans,), jnp.int32),
            pltpu.VMEM(strain.shape, F32),
            pltpu.VMEM(table.shape, BF16),
            pltpu.VMEM(twiddle.shape, F32),
            pltpu.SemaphoreType.DMA((5,)),
        ],
        compiler_params=pltpu.CompilerParams(vmem_limit_bytes=32 * MIB),
        cost_estimate=pl.CostEstimate(flops=6 * rows * samples * 2 * NF, bytes_accessed=4 * rows * samples, transcendentals=0),
        name="whiten",
    )(*[pltpu.with_memory_space_constraint(jnp.asarray(x), pltpu.HBM) for x in (alive, offset_limit, strain, table, twiddle)])


CHUNK = 4


def runs(octets, most):
    found = []
    for index, octet in enumerate(octets):
        if found and found[-1][1] + found[-1][2] == octet and found[-1][2] < most:
            found[-1][2] += 1
        else:
            found.append([index, octet, 1])
    return found


def correlate_kernel(places, needed, octets, early, wins, chans, share, lead, *refs):
    count = len(places)
    limit_ref = refs[0]
    blocks = refs[1 : count + 1]
    high_ref, low_ref = refs[count + 1 : count + 3]
    rest = refs[count + 3 :]
    early_ref = rest[0] if early else None
    out_ref, partner, x_high, x_low, lagged, out_sem, early_sem = rest[1 if early else 0 :]
    groups = partner.shape[0]
    place = lax.axis_index("win")
    half = TILES // 2

    def rows_of(first, length):
        return pl.ds(first * SUB, length * SUB)

    def early_stores():
        return [
            pltpu.make_async_copy(early_ref.at[rows_of(at, length)], out_ref.at[rows_of(octet, length)], early_sem.at[at])
            for at, octet, length in runs(early, len(early))
        ]

    def store(at, octet, length):
        target = out_ref.at[rows_of(octet if early else at, length)]
        return pltpu.make_async_copy(lagged.at[rows_of(at, length)], target, out_sem.at[at])

    pieces = runs(octets, CHUNK)

    def gather():
        chan, chan_count = lax.axis_index("chan"), lax.axis_size("chan")
        empty = {(steps, group) for steps in needed for group in range(groups)}
        for index in range(0 if lead else 1, count):
            for part, (steps, group) in enumerate(places[index]):
                if steps not in needed:
                    continue
                value = blocks[index][part]
                if lead and steps > 0:
                    value = jnp.where(chan + steps < chan_count, value, 0.0)
                first = needed.index(steps) * chans
                partner[group, :, :, first : first + chans, :] = value
                empty.remove((steps, group))
        for steps, group in sorted(empty):
            first = needed.index(steps) * chans
            partner[group, :, :, first : first + chans, :] = jnp.zeros((TILES, wins, chans, LANES), F32)

    def cross(octet):
        first = needed.index(octet) * SUB
        sums = [[jnp.zeros((chans, LANES), F32) for _ in range(TILES)] for _ in range(SUB)]
        for part, (_, group) in enumerate(places[0]):
            for w in range(wins):
                mine = [blocks[0][part, t, w] for t in range(TILES)]
                for j in range(SUB):
                    theirs = [partner[group, t, w, pl.ds(first + j + 1, SUB), :] for t in range(TILES)]
                    for t in range(half):
                        a_re, a_im, b_re, b_im = mine[t], mine[t + half], theirs[t], theirs[t + half]
                        sums[j][t] = sums[j][t] + (a_re * b_re + a_im * b_im)
                        sums[j][t + half] = sums[j][t + half] + (a_im * b_re - a_re * b_im)
        return sums

    def work():
        for copy in early_stores():
            copy.start()
        gather()
        limit = limit_ref[...]
        for at, octet, length in pieces:
            for k in range(length):
                sums = cross(octet + k)
                offset = place * share + (octet + k) * SUB
                for j in range(0, SUB, 2):
                    pair = [
                        jnp.concatenate([jnp.where(limit > offset + i, value, 0.0) for value in sums[i]], axis=1)
                        for i in (j, j + 1)
                    ]
                    high, low = halves(jnp.concatenate(pair, axis=0))
                    first = ((at + k) * SUB + j) * chans
                    x_high[first : first + 2 * chans, :] = high
                    x_low[first : first + 2 * chans, :] = low
            rows = slice(at * SUB * chans, (at + length) * SUB * chans)
            high, low = x_high[rows, :], x_low[rows, :]
            result = mm(high, high_ref[...]) + mm(high, low_ref[...]) + mm(low, high_ref[...])
            lagged[at * SUB : (at + length) * SUB] = result.reshape(length * SUB, chans, result.shape[1])
            store(at, octet, length).start()
        for copy in early_stores() + [store(*piece) for piece in pieces]:
            copy.wait()

    def blank():
        lagged[...] = jnp.zeros(lagged.shape, F32)
        copies = early_stores() + [store(*piece) for piece in pieces]
        for copy in copies:
            copy.start()
        for copy in copies:
            copy.wait()

    if lead:
        pl.when(place == 0)(work)
        pl.when(place != 0)(blank)
    else:
        work()


def correlate(given, octets, early, limit, wins, chans, share, samples, scale, lead):
    high, low = inverse_tables(samples, scale)
    needed = sorted({octet + step for octet in octets for step in (0, 1)})
    used = [item for index, item in enumerate(given) if index == 0 or any(steps in needed for steps, _ in item[1])]
    groups = len(given[0][1])
    size = len(octets) * SUB
    rows = size * chans
    lags = 2 * MAXLAG
    early_octets, early_result = early if early else ((), None)
    places = [item[1] for item in used]
    body = functools.partial(correlate_kernel, places, needed, octets, early_octets, wins, chans, share, lead)
    done = early is not None or len(octets) * SUB == share
    return pl.pallas_call(
        body,
        out_shape=jax.ShapeDtypeStruct((size + len(early_octets) * SUB, chans, lags), F32),
        in_specs=[pl.BlockSpec(memory_space=pltpu.VMEM)] * (len(used) + 3)
        + [pl.BlockSpec(memory_space=pl.ANY)] * bool(early),
        out_specs=pl.BlockSpec(memory_space=pl.ANY),
        scratch_shapes=[
            pltpu.VMEM((groups, TILES, wins, len(needed) * SUB, LANES), F32),
            pltpu.VMEM((rows, 2 * NF), BF16),
            pltpu.VMEM((rows, 2 * NF), BF16),
            pltpu.VMEM((size, chans, lags), F32),
            pltpu.SemaphoreType.DMA((len(octets),)),
            pltpu.SemaphoreType.DMA((max(1, len(early_octets)),)),
        ],
        compiler_params=pltpu.CompilerParams(vmem_limit_bytes=32 * MIB),
        cost_estimate=pl.CostEstimate(
            flops=6 * rows * 2 * NF * lags if done else 0,
            bytes_accessed=4 * rows * lags if done else 0,
            transcendentals=0,
        ),
        name="correlate",
    )(
        limit,
        *[block.reshape(-1, TILES, wins, chans, LANES) for block, _ in used],
        high,
        low,
        *([early_result] if early else []),
    )


def local(strain, offset_limit, alive):
    win_dev, ch_dev, samples = strain.shape
    win_count = lax.axis_size("win")
    chan_count = lax.axis_size("chan")
    scale = 1.0 / math.sqrt(NF * win_dev * win_count)
    share = MAXOFF // win_count
    reach = share // ch_dev
    axes = ("chan", "win")
    white, limit = whiten(strain, alive, offset_limit)
    finish = functools.partial(
        correlate,
        limit=limit,
        wins=win_dev,
        chans=ch_dev,
        share=share,
        samples=samples,
        scale=scale,
    )

    def device(chan, win):
        return chan * win_count + win

    def exchange(value, mask):
        pairs = [(device(c, w), device(c, w ^ mask)) for c in range(chan_count) for w in range(win_count)]
        return lax.ppermute(value, axes, pairs)

    def shift(wanted):
        sources = [w for w in range(win_count) if w not in [source for _, source in wanted.values()]]
        targets = [w for w in range(win_count) if w not in wanted]

        def cost(order):
            return sum(100 if s == t else (s ^ t) // 2 for s, t in zip(order, targets))

        idle = dict(zip(targets, min(itertools.permutations(sources), key=cost)))
        moves = {**wanted, **{target: (0, source) for target, source in idle.items()}}
        return [
            (device((c + steps) % chan_count, source), device(c, target))
            for target, (steps, source) in moves.items()
            for c in range(chan_count)
        ]

    if win_count == 4 and chan_count * ch_dev <= share:
        def held(steps, source, parts):
            return [(steps, source ^ part) for part in range(parts)]

        def join(value, mask):
            return jnp.concatenate([value, exchange(value, mask)], axis=0)

        chip = join(white, 1)
        far = [chan_count - 2, chan_count - 1] if chan_count >= 4 else []
        block = join(chip, 2)
        far_got = [lax.ppermute(chip, axes, shift({0: (steps, 3), 1: (steps, 1)})) for steps in reversed(far)][::-1]
        given = [(block, held(0, 0, 4))]
        last = chan_count - 1 - len(far)
        if chan_count > 1:
            given.append((lax.ppermute(block, axes, shift({0: (1, 1)})), held(1, 1, 4)))
        for even in range(2, last + 1, 2):
            wanted = {0: (even, 3)}
            if even + 1 <= last:
                wanted[1] = (even + 1, 1)
            got = lax.ppermute(block, axes, shift(wanted))
            given.append((got, held(even, 3, 4)))
            if even + 1 <= last:
                given.append((exchange(got, 1), held(even + 1, 1, 4)))
        if far:
            given += [(got, held(steps, 3, 2)) for got, steps in zip(far_got, far)]
            handed = exchange(jnp.concatenate(far_got, axis=0), 1)
            given.append((handed, [place for steps in far for place in held(steps, 1, 2)]))
        octets = range(reach)
        if not far:
            return finish(given, list(octets), None, lead=True)
        first = [octet for octet in octets if octet >= far[0]]
        early = first, finish(given, first, None, lead=True)
        return finish(given, [octet for octet in octets if octet < far[0]], early, lead=True)

    gathered = lax.all_gather(white, "win", tiled=True)

    def whole(steps):
        return [(steps, group) for group in range(win_count)]

    given = [(gathered, whole(0))]
    for steps in range(reach + 1):
        pairs = [
            (device(c + reach * w + steps, w), device(c, w))
            for w in range(win_count)
            for c in range(chan_count)
            if c + reach * w + steps < chan_count
        ]
        if pairs:
            given.append((lax.ppermute(gathered, axes, pairs), whole(steps)))
    return finish(given, list(range(reach)), None, lead=False)


def solution(mesh):
    in_specs = (P("win", "chan", None), P("chan"), P("chan"))
    out_specs = P("win", "chan", None)
    return jax.shard_map(local, mesh=mesh, in_specs=in_specs, out_specs=out_specs, check_vma=False)
```

```python
import functools
import itertools
import math

import jax
import jax.numpy as jnp
import ml_dtypes
import numpy as np
from jax import lax
from jax.experimental import pallas as pl
from jax.experimental.pallas import tpu as pltpu
from jax.sharding import PartitionSpec as P

NF = 256
MAXOFF = 256
MAXLAG = 200
EPS = 1e-06
WHITEN_BINS = 64
LANES = 128
SUB = 8
TILES = 2 * NF // LANES
BF16 = jnp.bfloat16
F32 = jnp.float32
MIB = 1 << 20


def split(table):
    high = table.astype(ml_dtypes.bfloat16)
    low = (table - high.astype(np.float64)).astype(ml_dtypes.bfloat16)
    return high, low


def phase(product, length):
    return (product % length) * (2.0 * math.pi / length)


def forward_tables(samples, chunk):
    freq = np.arange(1, NF + 1, dtype=np.int64)
    inner = phase(np.arange(chunk, dtype=np.int64)[:, None] * freq[None, :], samples)
    outer = phase(np.arange(samples // chunk, dtype=np.int64)[:, None] * chunk * freq[None, :], samples)
    twiddle = np.concatenate([np.cos(outer), np.sin(outer)], axis=1).astype(np.float32)
    return split(np.concatenate([np.cos(inner), -np.sin(inner)], axis=1)) + (twiddle,)


def inverse_tables(samples, scale):
    freq = np.arange(1, NF + 1, dtype=np.int64)
    lags = np.arange(-MAXLAG, MAXLAG, dtype=np.int64)
    angles = phase(freq[:, None] * lags[None, :], samples)
    return split(scale * np.concatenate([np.cos(angles), -np.sin(angles)], axis=0))


def halves(value):
    high = value.astype(BF16)
    return high, (value - high.astype(F32)).astype(BF16)


def mm(a, b):
    return jnp.dot(a, b, preferred_element_type=F32)


def column(ref, count):
    rows = lax.broadcasted_iota(jnp.int32, (count, LANES), 0)
    value = jnp.zeros((count, LANES), jnp.int32)
    for index in range(count):
        value = jnp.where(rows == index, ref[index], value)
    return value


def whiten_kernel(alive_hbm, limit_hbm, strain_hbm, table_hbm, twiddle_hbm, white_ref, limit_out, *scratch):
    alive_ref, limit_ref, strain_ref, table_ref, twiddle_ref, sems = scratch
    wins, chans, samples = strain_ref.shape
    chunk = table_ref.shape[0] // 2
    copies = [
        pltpu.make_async_copy(source, target, sems.at[index])
        for index, (source, target) in enumerate(
            [
                (strain_hbm, strain_ref),
                (table_hbm, table_ref),
                (twiddle_hbm, twiddle_ref),
                (alive_hbm, alive_ref),
                (limit_hbm, limit_ref),
            ]
        )
    ]
    for copy in copies:
        copy.start()
    block_r = lax.broadcasted_iota(jnp.int32, (NF, NF), 0) // WHITEN_BINS
    block_c = lax.broadcasted_iota(jnp.int32, (NF, NF), 1) // WHITEN_BINS
    mean = jnp.where(block_r == block_c, 1.0 / WHITEN_BINS, 0.0).astype(BF16)
    rows = wins * chans
    copies[0].wait()
    strain = strain_ref[...].reshape(rows, samples)
    pieces = samples // chunk
    stacked = jnp.concatenate([strain[:, a * chunk : (a + 1) * chunk] for a in range(pieces)], axis=0)
    x_high, x_low = halves(stacked)
    for copy in copies[1:]:
        copy.wait()
    high = table_ref[:chunk, :]
    part = mm(x_high, high) + mm(x_high, table_ref[chunk:, :]) + mm(x_low, high)
    real = jnp.zeros((rows, NF), F32)
    imag = jnp.zeros((rows, NF), F32)
    for a in range(pieces):
        p_re = part[a * rows : (a + 1) * rows, :NF]
        p_im = part[a * rows : (a + 1) * rows, NF:]
        cos = twiddle_ref[a : a + 1, :NF]
        sin = twiddle_ref[a : a + 1, NF:]
        real = real + p_re * cos + p_im * sin
        imag = imag + p_im * cos - p_re * sin
    magnitude = jnp.sqrt(real * real + imag * imag)
    m_high, m_low = halves(magnitude)
    level = mm(m_high, mean) + mm(m_low, mean) + EPS
    live = column(alive_ref, chans).astype(F32)
    limit_out[...] = column(limit_ref, chans)
    for w in range(wins):
        keep = slice(w * chans, (w + 1) * chans)
        for tile in range(TILES):
            source = real if tile < TILES // 2 else imag
            lanes = slice(tile % (TILES // 2) * LANES, (tile % (TILES // 2) + 1) * LANES)
            white_ref[(tile * wins + w) * chans : (tile * wins + w + 1) * chans, :] = (
                source[keep, lanes] / level[keep, lanes] * live
            )


def whiten(strain, alive, offset_limit):
    wins, chans, samples = strain.shape
    chunk = min(256, samples)
    high, low, twiddle = forward_tables(samples, chunk)
    table = np.concatenate([high, low], axis=0)
    rows = wins * chans
    return pl.pallas_call(
        whiten_kernel,
        out_shape=(
            jax.ShapeDtypeStruct((TILES * rows, LANES), F32),
            jax.ShapeDtypeStruct((chans, LANES), jnp.int32),
        ),
        in_specs=[pl.BlockSpec(memory_space=pltpu.HBM)] * 5,
        out_specs=(pl.BlockSpec(memory_space=pltpu.VMEM),) * 2,
        scratch_shapes=[
            pltpu.SMEM((chans,), jnp.int32),
            pltpu.SMEM((chans,), jnp.int32),
            pltpu.VMEM(strain.shape, F32),
            pltpu.VMEM(table.shape, BF16),
            pltpu.VMEM(twiddle.shape, F32),
            pltpu.SemaphoreType.DMA((5,)),
        ],
        compiler_params=pltpu.CompilerParams(vmem_limit_bytes=32 * MIB),
        cost_estimate=pl.CostEstimate(flops=6 * rows * samples * 2 * NF, bytes_accessed=4 * rows * samples, transcendentals=0),
        name="whiten",
    )(*[pltpu.with_memory_space_constraint(jnp.asarray(x), pltpu.HBM) for x in (alive, offset_limit, strain, table, twiddle)])


CHUNK = 4


def runs(octets, most):
    found = []
    for index, octet in enumerate(octets):
        if found and found[-1][1] + found[-1][2] == octet and found[-1][2] < most:
            found[-1][2] += 1
        else:
            found.append([index, octet, 1])
    return found


def correlate_kernel(places, needed, octets, early, wins, chans, share, lead, *refs):
    count = len(places)
    limit_ref = refs[0]
    blocks = refs[1 : count + 1]
    high_ref, low_ref = refs[count + 1 : count + 3]
    rest = refs[count + 3 :]
    early_ref = rest[0] if early else None
    out_ref, partner, x_high, x_low, lagged, out_sem, early_sem = rest[1 if early else 0 :]
    groups = partner.shape[0]
    place = lax.axis_index("win")
    half = TILES // 2

    def rows_of(first, length):
        return pl.ds(first * SUB, length * SUB)

    def early_stores():
        return [
            pltpu.make_async_copy(early_ref.at[rows_of(at, length)], out_ref.at[rows_of(octet, length)], early_sem.at[at])
            for at, octet, length in runs(early, len(early))
        ]

    def store(at, octet, length):
        target = out_ref.at[rows_of(octet if early else at, length)]
        return pltpu.make_async_copy(lagged.at[rows_of(at, length)], target, out_sem.at[at])

    pieces = runs(octets, CHUNK)

    def gather():
        chan, chan_count = lax.axis_index("chan"), lax.axis_size("chan")
        empty = {(steps, group) for steps in needed for group in range(groups)}
        for index in range(0 if lead else 1, count):
            for part, (steps, group) in enumerate(places[index]):
                if steps not in needed:
                    continue
                value = blocks[index][part]
                if lead and steps > 0:
                    value = jnp.where(chan + steps < chan_count, value, 0.0)
                first = needed.index(steps) * chans
                for t in range(half):
                    re, im = value[t], value[t + half]
                    partner[group, 3 * t, :, first : first + chans, :] = re
                    partner[group, 3 * t + 1, :, first : first + chans, :] = re + im
                    partner[group, 3 * t + 2, :, first : first + chans, :] = re - im
                empty.remove((steps, group))
        for steps, group in sorted(empty):
            first = needed.index(steps) * chans
            partner[group, :, :, first : first + chans, :] = jnp.zeros((3 * half, wins, chans, LANES), F32)

    def cross(octet):
        first = needed.index(octet) * SUB
        sums = [[jnp.zeros((chans, LANES), F32) for _ in range(3 * half)] for _ in range(SUB)]
        for part, (_, group) in enumerate(places[0]):
            for w in range(wins):
                for t in range(half):
                    a_re, a_im = blocks[0][part, t, w], blocks[0][part, t + half, w]
                    mine = (a_re + a_im, a_re, a_im)
                    for j in range(SUB):
                        for k in range(3):
                            theirs = partner[group, 3 * t + k, w, pl.ds(first + j + 1, SUB), :]
                            sums[j][3 * t + k] = sums[j][3 * t + k] + mine[k] * theirs
        return [
            [s[3 * t] - s[3 * t + 2] for t in range(half)] + [s[3 * t] - s[3 * t + 1] for t in range(half)] for s in sums
        ]

    def work():
        for copy in early_stores():
            copy.start()
        gather()
        limit = limit_ref[...]
        for at, octet, length in pieces:
            for k in range(length):
                sums = cross(octet + k)
                offset = place * share + (octet + k) * SUB
                for j in range(0, SUB, 2):
                    pair = [
                        jnp.concatenate([jnp.where(limit > offset + i, value, 0.0) for value in sums[i]], axis=1)
                        for i in (j, j + 1)
                    ]
                    high, low = halves(jnp.concatenate(pair, axis=0))
                    first = ((at + k) * SUB + j) * chans
                    x_high[first : first + 2 * chans, :] = high
                    x_low[first : first + 2 * chans, :] = low
            rows = slice(at * SUB * chans, (at + length) * SUB * chans)
            high, low = x_high[rows, :], x_low[rows, :]
            result = mm(high, high_ref[...]) + mm(high, low_ref[...]) + mm(low, high_ref[...])
            lagged[at * SUB : (at + length) * SUB] = result.reshape(length * SUB, chans, result.shape[1])
            store(at, octet, length).start()
        for copy in early_stores() + [store(*piece) for piece in pieces]:
            copy.wait()

    def blank():
        lagged[...] = jnp.zeros(lagged.shape, F32)
        copies = early_stores() + [store(*piece) for piece in pieces]
        for copy in copies:
            copy.start()
        for copy in copies:
            copy.wait()

    if lead:
        pl.when(place == 0)(work)
        pl.when(place != 0)(blank)
    else:
        work()


def correlate(given, octets, early, limit, wins, chans, share, samples, scale, lead):
    high, low = inverse_tables(samples, scale)
    needed = sorted({octet + step for octet in octets for step in (0, 1)})
    used = [item for index, item in enumerate(given) if index == 0 or any(steps in needed for steps, _ in item[1])]
    groups = len(given[0][1])
    size = len(octets) * SUB
    rows = size * chans
    lags = 2 * MAXLAG
    early_octets, early_result = early if early else ((), None)
    places = [item[1] for item in used]
    body = functools.partial(correlate_kernel, places, needed, octets, early_octets, wins, chans, share, lead)
    done = early is not None or len(octets) * SUB == share
    return pl.pallas_call(
        body,
        out_shape=jax.ShapeDtypeStruct((size + len(early_octets) * SUB, chans, lags), F32),
        in_specs=[pl.BlockSpec(memory_space=pltpu.VMEM)] * (len(used) + 3)
        + [pl.BlockSpec(memory_space=pl.ANY)] * bool(early),
        out_specs=pl.BlockSpec(memory_space=pl.ANY),
        scratch_shapes=[
            pltpu.VMEM((groups, 3 * TILES // 2, wins, len(needed) * SUB, LANES), F32),
            pltpu.VMEM((rows, 2 * NF), BF16),
            pltpu.VMEM((rows, 2 * NF), BF16),
            pltpu.VMEM((size, chans, lags), F32),
            pltpu.SemaphoreType.DMA((len(octets),)),
            pltpu.SemaphoreType.DMA((max(1, len(early_octets)),)),
        ],
        compiler_params=pltpu.CompilerParams(vmem_limit_bytes=32 * MIB),
        cost_estimate=pl.CostEstimate(
            flops=6 * rows * 2 * NF * lags if done else 0,
            bytes_accessed=4 * rows * lags if done else 0,
            transcendentals=0,
        ),
        name="correlate",
    )(
        limit,
        *[block.reshape(-1, TILES, wins, chans, LANES) for block, _ in used],
        high,
        low,
        *([early_result] if early else []),
    )


def local(strain, offset_limit, alive):
    win_dev, ch_dev, samples = strain.shape
    win_count = lax.axis_size("win")
    chan_count = lax.axis_size("chan")
    scale = 1.0 / math.sqrt(NF * win_dev * win_count)
    share = MAXOFF // win_count
    reach = share // ch_dev
    axes = ("chan", "win")
    white, limit = whiten(strain, alive, offset_limit)
    finish = functools.partial(
        correlate,
        limit=limit,
        wins=win_dev,
        chans=ch_dev,
        share=share,
        samples=samples,
        scale=scale,
    )

    def device(chan, win):
        return chan * win_count + win

    def exchange(value, mask):
        pairs = [(device(c, w), device(c, w ^ mask)) for c in range(chan_count) for w in range(win_count)]
        return lax.ppermute(value, axes, pairs)

    def shift(wanted):
        sources = [w for w in range(win_count) if w not in [source for _, source in wanted.values()]]
        targets = [w for w in range(win_count) if w not in wanted]

        def cost(order):
            return sum(100 if s == t else (s ^ t) // 2 for s, t in zip(order, targets))

        idle = dict(zip(targets, min(itertools.permutations(sources), key=cost)))
        moves = {**wanted, **{target: (0, source) for target, source in idle.items()}}
        return [
            (device((c + steps) % chan_count, source), device(c, target))
            for target, (steps, source) in moves.items()
            for c in range(chan_count)
        ]

    if win_count == 4 and chan_count * ch_dev <= share:
        def held(steps, source, parts):
            return [(steps, source ^ part) for part in range(parts)]

        def join(value, mask):
            return jnp.concatenate([value, exchange(value, mask)], axis=0)

        chip = join(white, 1)
        far = [chan_count - 2, chan_count - 1] if chan_count >= 4 else []
        block = join(chip, 2)
        far_got = [lax.ppermute(chip, axes, shift({0: (steps, 3), 1: (steps, 1)})) for steps in reversed(far)][::-1]
        given = [(block, held(0, 0, 4))]
        last = chan_count - 1 - len(far)
        if chan_count > 1:
            given.append((lax.ppermute(block, axes, shift({0: (1, 1)})), held(1, 1, 4)))
        for even in range(2, last + 1, 2):
            wanted = {0: (even, 3)}
            if even + 1 <= last:
                wanted[1] = (even + 1, 1)
            got = lax.ppermute(block, axes, shift(wanted))
            given.append((got, held(even, 3, 4)))
            if even + 1 <= last:
                given.append((exchange(got, 1), held(even + 1, 1, 4)))
        if far:
            given += [(got, held(steps, 3, 2)) for got, steps in zip(far_got, far)]
            handed = exchange(jnp.concatenate(far_got, axis=0), 1)
            given.append((handed, [place for steps in far for place in held(steps, 1, 2)]))
        octets = range(reach)
        if not far:
            return finish(given, list(octets), None, lead=True)
        first = [octet for octet in octets if octet >= far[0]]
        early = first, finish(given, first, None, lead=True)
        return finish(given, [octet for octet in octets if octet < far[0]], early, lead=True)

    gathered = lax.all_gather(white, "win", tiled=True)

    def whole(steps):
        return [(steps, group) for group in range(win_count)]

    given = [(gathered, whole(0))]
    for steps in range(reach + 1):
        pairs = [
            (device(c + reach * w + steps, w), device(c, w))
            for w in range(win_count)
            for c in range(chan_count)
            if c + reach * w + steps < chan_count
        ]
        if pairs:
            given.append((lax.ppermute(gathered, axes, pairs), whole(steps)))
    return finish(given, list(range(reach)), None, lead=False)


def solution(mesh):
    in_specs = (P("win", "chan", None), P("chan"), P("chan"))
    out_specs = P("win", "chan", None)
    return jax.shard_map(local, mesh=mesh, in_specs=in_specs, out_specs=out_specs, check_vma=False)
```

```python
import functools
import itertools
import math

import jax
import jax.numpy as jnp
import ml_dtypes
import numpy as np
from jax import lax
from jax.experimental import pallas as pl
from jax.experimental.pallas import tpu as pltpu
from jax.sharding import PartitionSpec as P

NF = 256
MAXOFF = 256
MAXLAG = 200
EPS = 1e-06
WHITEN_BINS = 64
LANES = 128
SUB = 8
TILES = 2 * NF // LANES
BF16 = jnp.bfloat16
F32 = jnp.float32
MIB = 1 << 20


def split(table):
    high = table.astype(ml_dtypes.bfloat16)
    low = (table - high.astype(np.float64)).astype(ml_dtypes.bfloat16)
    return high, low


def phase(product, length):
    return (product % length) * (2.0 * math.pi / length)


def forward_tables(samples, chunk):
    freq = np.arange(1, NF + 1, dtype=np.int64)
    inner = phase(np.arange(chunk, dtype=np.int64)[:, None] * freq[None, :], samples)
    outer = phase(np.arange(samples // chunk, dtype=np.int64)[:, None] * chunk * freq[None, :], samples)
    twiddle = np.concatenate([np.cos(outer), np.sin(outer)], axis=1).astype(np.float32)
    return split(np.concatenate([np.cos(inner), -np.sin(inner)], axis=1)) + (twiddle,)


def inverse_tables(samples, scale):
    freq = np.arange(1, NF + 1, dtype=np.int64)
    lags = np.arange(-MAXLAG, MAXLAG, dtype=np.int64)
    angles = phase(freq[:, None] * lags[None, :], samples)
    return split(scale * np.concatenate([np.cos(angles), -np.sin(angles)], axis=0))


def halves(value):
    high = value.astype(BF16)
    return high, (value - high.astype(F32)).astype(BF16)


def mm(a, b):
    return jnp.dot(a, b, preferred_element_type=F32)


def column(ref, count):
    rows = lax.broadcasted_iota(jnp.int32, (count, LANES), 0)
    value = jnp.zeros((count, LANES), jnp.int32)
    for index in range(count):
        value = jnp.where(rows == index, ref[index], value)
    return value


def whiten_kernel(alive_hbm, limit_hbm, strain_hbm, table_hbm, twiddle_hbm, white_ref, limit_out, *scratch):
    alive_ref, limit_ref, strain_ref, table_ref, twiddle_ref, sems = scratch
    wins, chans, samples = strain_ref.shape
    chunk = table_ref.shape[0] // 2
    copies = [
        pltpu.make_async_copy(source, target, sems.at[index])
        for index, (source, target) in enumerate(
            [
                (strain_hbm, strain_ref),
                (table_hbm, table_ref),
                (twiddle_hbm, twiddle_ref),
                (alive_hbm, alive_ref),
                (limit_hbm, limit_ref),
            ]
        )
    ]
    for copy in copies:
        copy.start()
    block_r = lax.broadcasted_iota(jnp.int32, (NF, NF), 0) // WHITEN_BINS
    block_c = lax.broadcasted_iota(jnp.int32, (NF, NF), 1) // WHITEN_BINS
    mean = jnp.where(block_r == block_c, 1.0 / WHITEN_BINS, 0.0).astype(BF16)
    rows = wins * chans
    copies[0].wait()
    strain = strain_ref[...].reshape(rows, samples)
    pieces = samples // chunk
    stacked = jnp.concatenate([strain[:, a * chunk : (a + 1) * chunk] for a in range(pieces)], axis=0)
    x_high, x_low = halves(stacked)
    for copy in copies[1:]:
        copy.wait()
    high = table_ref[:chunk, :]
    part = mm(x_high, high) + mm(x_high, table_ref[chunk:, :]) + mm(x_low, high)
    real = jnp.zeros((rows, NF), F32)
    imag = jnp.zeros((rows, NF), F32)
    for a in range(pieces):
        p_re = part[a * rows : (a + 1) * rows, :NF]
        p_im = part[a * rows : (a + 1) * rows, NF:]
        cos = twiddle_ref[a : a + 1, :NF]
        sin = twiddle_ref[a : a + 1, NF:]
        real = real + p_re * cos + p_im * sin
        imag = imag + p_im * cos - p_re * sin
    magnitude = jnp.sqrt(real * real + imag * imag)
    m_high, m_low = halves(magnitude)
    level = mm(m_high, mean) + mm(m_low, mean) + EPS
    live = column(alive_ref, chans).astype(F32)
    limit_out[...] = column(limit_ref, chans)
    for w in range(wins):
        keep = slice(w * chans, (w + 1) * chans)
        for tile in range(TILES):
            source = real if tile < TILES // 2 else imag
            lanes = slice(tile % (TILES // 2) * LANES, (tile % (TILES // 2) + 1) * LANES)
            white_ref[(tile * wins + w) * chans : (tile * wins + w + 1) * chans, :] = (
                source[keep, lanes] / level[keep, lanes] * live
            )


def whiten(strain, alive, offset_limit):
    wins, chans, samples = strain.shape
    chunk = min(256, samples)
    high, low, twiddle = forward_tables(samples, chunk)
    table = np.concatenate([high, low], axis=0)
    rows = wins * chans
    return pl.pallas_call(
        whiten_kernel,
        out_shape=(
            jax.ShapeDtypeStruct((TILES * rows, LANES), F32),
            jax.ShapeDtypeStruct((chans, LANES), jnp.int32),
        ),
        in_specs=[pl.BlockSpec(memory_space=pltpu.HBM)] * 5,
        out_specs=(pl.BlockSpec(memory_space=pltpu.VMEM),) * 2,
        scratch_shapes=[
            pltpu.SMEM((chans,), jnp.int32),
            pltpu.SMEM((chans,), jnp.int32),
            pltpu.VMEM(strain.shape, F32),
            pltpu.VMEM(table.shape, BF16),
            pltpu.VMEM(twiddle.shape, F32),
            pltpu.SemaphoreType.DMA((5,)),
        ],
        compiler_params=pltpu.CompilerParams(vmem_limit_bytes=32 * MIB),
        cost_estimate=pl.CostEstimate(flops=6 * rows * samples * 2 * NF, bytes_accessed=4 * rows * samples, transcendentals=0),
        name="whiten",
    )(*[pltpu.with_memory_space_constraint(jnp.asarray(x), pltpu.HBM) for x in (alive, offset_limit, strain, table, twiddle)])


CHUNK = 4


def runs(octets, most):
    found = []
    for index, octet in enumerate(octets):
        if found and found[-1][1] + found[-1][2] == octet and found[-1][2] < most:
            found[-1][2] += 1
        else:
            found.append([index, octet, 1])
    return found


def correlate_kernel(places, needed, octets, early, wins, chans, share, lead, *refs):
    count = len(places)
    limit_ref = refs[0]
    blocks = refs[1 : count + 1]
    high_ref, low_ref = refs[count + 1 : count + 3]
    rest = refs[count + 3 :]
    early_ref = rest[0] if early else None
    out_ref, partner, x_high, x_low, lagged, out_sem, early_sem = rest[1 if early else 0 :]
    groups = partner.shape[0]
    place = lax.axis_index("win")
    half = TILES // 2

    def rows_of(first, length):
        return pl.ds(first * SUB, length * SUB)

    def early_stores():
        return [
            pltpu.make_async_copy(early_ref.at[rows_of(at, length)], out_ref.at[rows_of(octet, length)], early_sem.at[at])
            for at, octet, length in runs(early, len(early))
        ]

    def store(at, octet, length):
        target = out_ref.at[rows_of(octet if early else at, length)]
        return pltpu.make_async_copy(lagged.at[rows_of(at, length)], target, out_sem.at[at])

    pieces = runs(octets, CHUNK)

    def gather():
        chan, chan_count = lax.axis_index("chan"), lax.axis_size("chan")
        empty = {(steps, group) for steps in needed for group in range(groups)}
        for index in range(0 if lead else 1, count):
            for part, (steps, group) in enumerate(places[index]):
                if steps not in needed:
                    continue
                value = blocks[index][part]
                if lead and steps > 0:
                    value = jnp.where(chan + steps < chan_count, value, 0.0)
                first = needed.index(steps) * chans
                for t in range(half):
                    re, im = value[t], value[t + half]
                    partner[group, 3 * t, :, first : first + chans, :] = re
                    partner[group, 3 * t + 1, :, first : first + chans, :] = re + im
                    partner[group, 3 * t + 2, :, first : first + chans, :] = re - im
                empty.remove((steps, group))
        for steps, group in sorted(empty):
            first = needed.index(steps) * chans
            partner[group, :, :, first : first + chans, :] = jnp.zeros((3 * half, wins, chans, LANES), F32)

    def cross(octet):
        first = needed.index(octet) * SUB
        sums = [[jnp.zeros((chans, LANES), F32) for _ in range(3 * half)] for _ in range(SUB)]
        for part, (_, group) in enumerate(places[0]):
            for w in range(wins):
                for t in range(half):
                    a_re, a_im = blocks[0][part, t, w], blocks[0][part, t + half, w]
                    mine = (a_re + a_im, a_re, a_im)
                    for j in range(SUB):
                        for k in range(3):
                            theirs = partner[group, 3 * t + k, w, pl.ds(first + j + 1, SUB), :]
                            sums[j][3 * t + k] = sums[j][3 * t + k] + mine[k] * theirs
        return [
            [s[3 * t] - s[3 * t + 2] for t in range(half)] + [s[3 * t] - s[3 * t + 1] for t in range(half)] for s in sums
        ]

    def work():
        for copy in early_stores():
            copy.start()
        gather()
        limit = limit_ref[...]
        for at, octet, length in pieces:
            for k in range(length):
                sums = cross(octet + k)
                offset = place * share + (octet + k) * SUB
                for j in range(0, SUB, 2):
                    pair = [
                        jnp.concatenate([jnp.where(limit > offset + i, value, 0.0) for value in sums[i]], axis=1)
                        for i in (j, j + 1)
                    ]
                    high, low = halves(jnp.concatenate(pair, axis=0))
                    first = ((at + k) * SUB + j) * chans
                    x_high[first : first + 2 * chans, :] = high
                    x_low[first : first + 2 * chans, :] = low
            rows = slice(at * SUB * chans, (at + length) * SUB * chans)
            high, low = x_high[rows, :], x_low[rows, :]
            result = mm(high, high_ref[...]) + mm(high, low_ref[...]) + mm(low, high_ref[...])
            lagged[at * SUB : (at + length) * SUB] = result.reshape(length * SUB, chans, result.shape[1])
            store(at, octet, length).start()
        for copy in early_stores() + [store(*piece) for piece in pieces]:
            copy.wait()

    def blank():
        lagged[...] = jnp.zeros(lagged.shape, F32)
        copies = early_stores() + [store(*piece) for piece in pieces]
        for copy in copies:
            copy.start()
        for copy in copies:
            copy.wait()

    if lead:
        pl.when(place == 0)(work)
        pl.when(place != 0)(blank)
    else:
        work()


def correlate(given, octets, early, limit, wins, chans, share, samples, scale, lead):
    high, low = inverse_tables(samples, scale)
    needed = sorted({octet + step for octet in octets for step in (0, 1)})
    used = [item for index, item in enumerate(given) if index == 0 or any(steps in needed for steps, _ in item[1])]
    groups = len(given[0][1])
    size = len(octets) * SUB
    rows = size * chans
    lags = 2 * MAXLAG
    early_octets, early_result = early if early else ((), None)
    places = [item[1] for item in used]
    body = functools.partial(correlate_kernel, places, needed, octets, early_octets, wins, chans, share, lead)
    done = early is not None or len(octets) * SUB == share
    return pl.pallas_call(
        body,
        out_shape=jax.ShapeDtypeStruct((size + len(early_octets) * SUB, chans, lags), F32),
        in_specs=[pl.BlockSpec(memory_space=pltpu.VMEM)] * (len(used) + 3)
        + [pl.BlockSpec(memory_space=pl.ANY)] * bool(early),
        out_specs=pl.BlockSpec(memory_space=pl.ANY),
        scratch_shapes=[
            pltpu.VMEM((groups, 3 * TILES // 2, wins, len(needed) * SUB, LANES), F32),
            pltpu.VMEM((rows, 2 * NF), BF16),
            pltpu.VMEM((rows, 2 * NF), BF16),
            pltpu.VMEM((size, chans, lags), F32),
            pltpu.SemaphoreType.DMA((len(octets),)),
            pltpu.SemaphoreType.DMA((max(1, len(early_octets)),)),
        ],
        compiler_params=pltpu.CompilerParams(vmem_limit_bytes=32 * MIB),
        cost_estimate=pl.CostEstimate(
            flops=6 * rows * 2 * NF * lags if done else 0,
            bytes_accessed=4 * rows * lags if done else 0,
            transcendentals=0,
        ),
        name="correlate",
    )(
        limit,
        *[block.reshape(-1, TILES, wins, chans, LANES) for block, _ in used],
        high,
        low,
        *([early_result] if early else []),
    )


def local(strain, offset_limit, alive):
    win_dev, ch_dev, samples = strain.shape
    win_count = lax.axis_size("win")
    chan_count = lax.axis_size("chan")
    scale = 1.0 / math.sqrt(NF * win_dev * win_count)
    share = MAXOFF // win_count
    reach = share // ch_dev
    axes = ("chan", "win")
    white, limit = whiten(strain, alive, offset_limit)
    finish = functools.partial(
        correlate,
        limit=limit,
        wins=win_dev,
        chans=ch_dev,
        share=share,
        samples=samples,
        scale=scale,
    )

    def device(chan, win):
        return chan * win_count + win

    def exchange(value, mask):
        pairs = [(device(c, w), device(c, w ^ mask)) for c in range(chan_count) for w in range(win_count)]
        return lax.ppermute(value, axes, pairs)

    def shift(wanted):
        sources = [w for w in range(win_count) if w not in [source for _, source in wanted.values()]]
        targets = [w for w in range(win_count) if w not in wanted]

        def cost(order):
            return sum(100 if s == t else (s ^ t) // 2 for s, t in zip(order, targets))

        idle = dict(zip(targets, min(itertools.permutations(sources), key=cost)))
        moves = {**wanted, **{target: (0, source) for target, source in idle.items()}}
        return [
            (device((c + steps) % chan_count, source), device(c, target))
            for target, (steps, source) in moves.items()
            for c in range(chan_count)
        ]

    if win_count == 4 and chan_count * ch_dev <= share:
        def held(steps, source, parts):
            return [(steps, source ^ part) for part in range(parts)]

        def join(value, mask):
            return jnp.concatenate([value, exchange(value, mask)], axis=0)

        chip = join(white, 1)
        far = [chan_count - 2, chan_count - 1] if chan_count >= 4 else []
        block = join(chip, 2)
        far_got = [lax.ppermute(chip, axes, shift({0: (steps, 1), 1: (steps, 3)})) for steps in reversed(far)][::-1]
        given = [(block, held(0, 0, 4))]
        last = chan_count - 1 - len(far)
        if chan_count > 1:
            given.append((lax.ppermute(block, axes, shift({0: (1, 1)})), held(1, 1, 4)))
        for even in range(2, last + 1, 2):
            wanted = {0: (even, 3)}
            if even + 1 <= last:
                wanted[1] = (even + 1, 1)
            got = lax.ppermute(block, axes, shift(wanted))
            given.append((got, held(even, 3, 4)))
            if even + 1 <= last:
                given.append((exchange(got, 1), held(even + 1, 1, 4)))
        if far:
            given += [(got, held(steps, 1, 2)) for got, steps in zip(far_got, far)]
            handed = exchange(jnp.concatenate(far_got, axis=0), 1)
            given.append((handed, [place for steps in far for place in held(steps, 3, 2)]))
        octets = range(reach)
        if not far:
            return finish(given, list(octets), None, lead=True)
        first = [octet for octet in octets if octet >= far[0]]
        early = first, finish(given, first, None, lead=True)
        return finish(given, [octet for octet in octets if octet < far[0]], early, lead=True)

    gathered = lax.all_gather(white, "win", tiled=True)

    def whole(steps):
        return [(steps, group) for group in range(win_count)]

    given = [(gathered, whole(0))]
    for steps in range(reach + 1):
        pairs = [
            (device(c + reach * w + steps, w), device(c, w))
            for w in range(win_count)
            for c in range(chan_count)
            if c + reach * w + steps < chan_count
        ]
        if pairs:
            given.append((lax.ppermute(gathered, axes, pairs), whole(steps)))
    return finish(given, list(range(reach)), None, lead=False)


def solution(mesh):
    in_specs = (P("win", "chan", None), P("chan"), P("chan"))
    out_specs = P("win", "chan", None)
    return jax.shard_map(local, mesh=mesh, in_specs=in_specs, out_specs=out_specs, check_vma=False)
```

```python
import functools
import itertools
import math

import jax
import jax.numpy as jnp
import ml_dtypes
import numpy as np
from jax import lax
from jax.experimental import pallas as pl
from jax.experimental.pallas import tpu as pltpu
from jax.sharding import PartitionSpec as P

NF = 256
MAXOFF = 256
MAXLAG = 200
EPS = 1e-06
WHITEN_BINS = 64
LANES = 128
SUB = 8
TILES = 2 * NF // LANES
BF16 = jnp.bfloat16
F32 = jnp.float32
MIB = 1 << 20


def split(table):
    high = table.astype(ml_dtypes.bfloat16)
    low = (table - high.astype(np.float64)).astype(ml_dtypes.bfloat16)
    return high, low


def phase(product, length):
    return (product % length) * (2.0 * math.pi / length)


def forward_tables(samples, chunk):
    freq = np.arange(1, NF + 1, dtype=np.int64)
    inner = phase(np.arange(chunk, dtype=np.int64)[:, None] * freq[None, :], samples)
    outer = phase(np.arange(samples // chunk, dtype=np.int64)[:, None] * chunk * freq[None, :], samples)
    twiddle = np.concatenate([np.cos(outer), np.sin(outer)], axis=1).astype(np.float32)
    return split(np.concatenate([np.cos(inner), -np.sin(inner)], axis=1)) + (twiddle,)


def inverse_tables(samples, scale):
    freq = np.arange(1, NF + 1, dtype=np.int64)
    lags = np.arange(-MAXLAG, MAXLAG, dtype=np.int64)
    angles = phase(freq[:, None] * lags[None, :], samples)
    return split(scale * np.concatenate([np.cos(angles), -np.sin(angles)], axis=0))


def halves(value):
    high = value.astype(BF16)
    return high, (value - high.astype(F32)).astype(BF16)


def mm(a, b):
    return jnp.dot(a, b, preferred_element_type=F32)


def column(ref, count):
    rows = lax.broadcasted_iota(jnp.int32, (count, LANES), 0)
    value = jnp.zeros((count, LANES), jnp.int32)
    for index in range(count):
        value = jnp.where(rows == index, ref[index], value)
    return value


def whiten_kernel(alive_hbm, limit_hbm, strain_hbm, table_hbm, twiddle_hbm, white_ref, limit_out, *scratch):
    alive_ref, limit_ref, strain_ref, table_ref, twiddle_ref, sems = scratch
    wins, chans, samples = strain_ref.shape
    chunk = table_ref.shape[0] // 2
    copies = [
        pltpu.make_async_copy(source, target, sems.at[index])
        for index, (source, target) in enumerate(
            [
                (strain_hbm, strain_ref),
                (table_hbm, table_ref),
                (twiddle_hbm, twiddle_ref),
                (alive_hbm, alive_ref),
                (limit_hbm, limit_ref),
            ]
        )
    ]
    for copy in copies:
        copy.start()
    block_r = lax.broadcasted_iota(jnp.int32, (NF, NF), 0) // WHITEN_BINS
    block_c = lax.broadcasted_iota(jnp.int32, (NF, NF), 1) // WHITEN_BINS
    mean = jnp.where(block_r == block_c, 1.0 / WHITEN_BINS, 0.0).astype(BF16)
    rows = wins * chans
    copies[0].wait()
    strain = strain_ref[...].reshape(rows, samples)
    pieces = samples // chunk
    stacked = jnp.concatenate([strain[:, a * chunk : (a + 1) * chunk] for a in range(pieces)], axis=0)
    x_high, x_low = halves(stacked)
    for copy in copies[1:]:
        copy.wait()
    high = table_ref[:chunk, :]
    table = jnp.concatenate([high, table_ref[chunk:, :], high], axis=0)
    part = mm(jnp.concatenate([x_high, x_high, x_low], axis=1), table)
    real = jnp.zeros((rows, NF), F32)
    imag = jnp.zeros((rows, NF), F32)
    for a in range(pieces):
        p_re = part[a * rows : (a + 1) * rows, :NF]
        p_im = part[a * rows : (a + 1) * rows, NF:]
        cos = twiddle_ref[a : a + 1, :NF]
        sin = twiddle_ref[a : a + 1, NF:]
        real = real + p_re * cos + p_im * sin
        imag = imag + p_im * cos - p_re * sin
    magnitude = jnp.sqrt(real * real + imag * imag)
    m_high, m_low = halves(magnitude)
    level = mm(m_high, mean) + mm(m_low, mean) + EPS
    live = column(alive_ref, chans).astype(F32)
    limit_out[...] = column(limit_ref, chans)
    for w in range(wins):
        keep = slice(w * chans, (w + 1) * chans)
        for tile in range(TILES):
            source = real if tile < TILES // 2 else imag
            lanes = slice(tile % (TILES // 2) * LANES, (tile % (TILES // 2) + 1) * LANES)
            white_ref[(tile * wins + w) * chans : (tile * wins + w + 1) * chans, :] = (
                source[keep, lanes] / level[keep, lanes] * live
            )


def whiten(strain, alive, offset_limit):
    wins, chans, samples = strain.shape
    chunk = min(256, samples)
    high, low, twiddle = forward_tables(samples, chunk)
    table = np.concatenate([high, low], axis=0)
    rows = wins * chans
    return pl.pallas_call(
        whiten_kernel,
        out_shape=(
            jax.ShapeDtypeStruct((TILES * rows, LANES), F32),
            jax.ShapeDtypeStruct((chans, LANES), jnp.int32),
        ),
        in_specs=[pl.BlockSpec(memory_space=pltpu.HBM)] * 5,
        out_specs=(pl.BlockSpec(memory_space=pltpu.VMEM),) * 2,
        scratch_shapes=[
            pltpu.SMEM((chans,), jnp.int32),
            pltpu.SMEM((chans,), jnp.int32),
            pltpu.VMEM(strain.shape, F32),
            pltpu.VMEM(table.shape, BF16),
            pltpu.VMEM(twiddle.shape, F32),
            pltpu.SemaphoreType.DMA((5,)),
        ],
        compiler_params=pltpu.CompilerParams(vmem_limit_bytes=32 * MIB),
        cost_estimate=pl.CostEstimate(flops=6 * rows * samples * 2 * NF, bytes_accessed=4 * rows * samples, transcendentals=0),
        name="whiten",
    )(*[pltpu.with_memory_space_constraint(jnp.asarray(x), pltpu.HBM) for x in (alive, offset_limit, strain, table, twiddle)])


CHUNK = 4


def runs(octets, most):
    found = []
    for index, octet in enumerate(octets):
        if found and found[-1][1] + found[-1][2] == octet and found[-1][2] < most:
            found[-1][2] += 1
        else:
            found.append([index, octet, 1])
    return found


def correlate_kernel(places, needed, octets, early, wins, chans, share, lead, *refs):
    count = len(places)
    limit_ref = refs[0]
    blocks = refs[1 : count + 1]
    high_ref, low_ref = refs[count + 1 : count + 3]
    rest = refs[count + 3 :]
    early_ref = rest[0] if early else None
    out_ref, partner, x_high, x_low, lagged, out_sem, early_sem = rest[1 if early else 0 :]
    groups = partner.shape[0]
    place = lax.axis_index("win")
    half = TILES // 2

    def rows_of(first, length):
        return pl.ds(first * SUB, length * SUB)

    def early_stores():
        return [
            pltpu.make_async_copy(early_ref.at[rows_of(at, length)], out_ref.at[rows_of(octet, length)], early_sem.at[at])
            for at, octet, length in runs(early, len(early))
        ]

    def store(at, octet, length):
        target = out_ref.at[rows_of(octet if early else at, length)]
        return pltpu.make_async_copy(lagged.at[rows_of(at, length)], target, out_sem.at[at])

    pieces = runs(octets, CHUNK)

    def gather():
        chan, chan_count = lax.axis_index("chan"), lax.axis_size("chan")
        empty = {(steps, group) for steps in needed for group in range(groups)}
        for index in range(0 if lead else 1, count):
            for part, (steps, group) in enumerate(places[index]):
                if steps not in needed:
                    continue
                value = blocks[index][part]
                if lead and steps > 0:
                    value = jnp.where(chan + steps < chan_count, value, 0.0)
                first = needed.index(steps) * chans
                for t in range(half):
                    re, im = value[t], value[t + half]
                    partner[group, 3 * t, :, first : first + chans, :] = re
                    partner[group, 3 * t + 1, :, first : first + chans, :] = re + im
                    partner[group, 3 * t + 2, :, first : first + chans, :] = re - im
                empty.remove((steps, group))
        for steps, group in sorted(empty):
            first = needed.index(steps) * chans
            partner[group, :, :, first : first + chans, :] = jnp.zeros((3 * half, wins, chans, LANES), F32)

    def cross(octet):
        first = needed.index(octet) * SUB
        sums = [[jnp.zeros((chans, LANES), F32) for _ in range(3 * half)] for _ in range(SUB)]
        for part, (_, group) in enumerate(places[0]):
            for w in range(wins):
                for t in range(half):
                    a_re, a_im = blocks[0][part, t, w], blocks[0][part, t + half, w]
                    mine = (a_re + a_im, a_re, a_im)
                    for j in range(SUB):
                        for k in range(3):
                            theirs = partner[group, 3 * t + k, w, pl.ds(first + j + 1, SUB), :]
                            sums[j][3 * t + k] = sums[j][3 * t + k] + mine[k] * theirs
        return [
            [s[3 * t] - s[3 * t + 2] for t in range(half)] + [s[3 * t] - s[3 * t + 1] for t in range(half)] for s in sums
        ]

    def work():
        for copy in early_stores():
            copy.start()
        gather()
        limit = limit_ref[...]
        for at, octet, length in pieces:
            for k in range(length):
                sums = cross(octet + k)
                offset = place * share + (octet + k) * SUB
                for j in range(0, SUB, 2):
                    pair = [
                        jnp.concatenate([jnp.where(limit > offset + i, value, 0.0) for value in sums[i]], axis=1)
                        for i in (j, j + 1)
                    ]
                    high, low = halves(jnp.concatenate(pair, axis=0))
                    first = ((at + k) * SUB + j) * chans
                    x_high[first : first + 2 * chans, :] = high
                    x_low[first : first + 2 * chans, :] = low
            rows = slice(at * SUB * chans, (at + length) * SUB * chans)
            high, low = x_high[rows, :], x_low[rows, :]
            table = jnp.concatenate([high_ref[...], low_ref[...], high_ref[...]], axis=0)
            result = mm(jnp.concatenate([high, high, low], axis=1), table)
            lagged[at * SUB : (at + length) * SUB] = result.reshape(length * SUB, chans, result.shape[1])
            store(at, octet, length).start()
        for copy in early_stores() + [store(*piece) for piece in pieces]:
            copy.wait()

    def blank():
        lagged[...] = jnp.zeros(lagged.shape, F32)
        copies = early_stores() + [store(*piece) for piece in pieces]
        for copy in copies:
            copy.start()
        for copy in copies:
            copy.wait()

    if lead:
        pl.when(place == 0)(work)
        pl.when(place != 0)(blank)
    else:
        work()


def correlate(given, octets, early, limit, wins, chans, share, samples, scale, lead):
    high, low = inverse_tables(samples, scale)
    needed = sorted({octet + step for octet in octets for step in (0, 1)})
    used = [item for index, item in enumerate(given) if index == 0 or any(steps in needed for steps, _ in item[1])]
    groups = len(given[0][1])
    size = len(octets) * SUB
    rows = size * chans
    lags = 2 * MAXLAG
    early_octets, early_result = early if early else ((), None)
    places = [item[1] for item in used]
    body = functools.partial(correlate_kernel, places, needed, octets, early_octets, wins, chans, share, lead)
    done = early is not None or len(octets) * SUB == share
    return pl.pallas_call(
        body,
        out_shape=jax.ShapeDtypeStruct((size + len(early_octets) * SUB, chans, lags), F32),
        in_specs=[pl.BlockSpec(memory_space=pltpu.VMEM)] * (len(used) + 3)
        + [pl.BlockSpec(memory_space=pl.ANY)] * bool(early),
        out_specs=pl.BlockSpec(memory_space=pl.ANY),
        scratch_shapes=[
            pltpu.VMEM((groups, 3 * TILES // 2, wins, len(needed) * SUB, LANES), F32),
            pltpu.VMEM((rows, 2 * NF), BF16),
            pltpu.VMEM((rows, 2 * NF), BF16),
            pltpu.VMEM((size, chans, lags), F32),
            pltpu.SemaphoreType.DMA((len(octets),)),
            pltpu.SemaphoreType.DMA((max(1, len(early_octets)),)),
        ],
        compiler_params=pltpu.CompilerParams(vmem_limit_bytes=32 * MIB),
        cost_estimate=pl.CostEstimate(
            flops=6 * rows * 2 * NF * lags if done else 0,
            bytes_accessed=4 * rows * lags if done else 0,
            transcendentals=0,
        ),
        name="correlate",
    )(
        limit,
        *[block.reshape(-1, TILES, wins, chans, LANES) for block, _ in used],
        high,
        low,
        *([early_result] if early else []),
    )


def local(strain, offset_limit, alive):
    win_dev, ch_dev, samples = strain.shape
    win_count = lax.axis_size("win")
    chan_count = lax.axis_size("chan")
    scale = 1.0 / math.sqrt(NF * win_dev * win_count)
    share = MAXOFF // win_count
    reach = share // ch_dev
    axes = ("chan", "win")
    white, limit = whiten(strain, alive, offset_limit)
    finish = functools.partial(
        correlate,
        limit=limit,
        wins=win_dev,
        chans=ch_dev,
        share=share,
        samples=samples,
        scale=scale,
    )

    def device(chan, win):
        return chan * win_count + win

    def exchange(value, mask):
        pairs = [(device(c, w), device(c, w ^ mask)) for c in range(chan_count) for w in range(win_count)]
        return lax.ppermute(value, axes, pairs)

    def shift(wanted):
        sources = [w for w in range(win_count) if w not in [source for _, source in wanted.values()]]
        targets = [w for w in range(win_count) if w not in wanted]

        def cost(order):
            return sum(100 if s == t else (s ^ t) // 2 for s, t in zip(order, targets))

        idle = dict(zip(targets, min(itertools.permutations(sources), key=cost)))
        moves = {**wanted, **{target: (0, source) for target, source in idle.items()}}
        return [
            (device((c + steps) % chan_count, source), device(c, target))
            for target, (steps, source) in moves.items()
            for c in range(chan_count)
        ]

    if win_count == 4 and chan_count * ch_dev <= share:
        def held(steps, source, parts):
            return [(steps, source ^ part) for part in range(parts)]

        def join(value, mask):
            return jnp.concatenate([value, exchange(value, mask)], axis=0)

        chip = join(white, 1)
        far = [chan_count - 2, chan_count - 1] if chan_count >= 4 else []
        block = join(chip, 2)
        far_got = [lax.ppermute(chip, axes, shift({0: (steps, 1), 1: (steps, 3)})) for steps in reversed(far)][::-1]
        given = [(block, held(0, 0, 4))]
        last = chan_count - 1 - len(far)
        if chan_count > 1:
            given.append((lax.ppermute(block, axes, shift({0: (1, 1)})), held(1, 1, 4)))
        for even in range(2, last + 1, 2):
            wanted = {0: (even, 3)}
            if even + 1 <= last:
                wanted[1] = (even + 1, 1)
            got = lax.ppermute(block, axes, shift(wanted))
            given.append((got, held(even, 3, 4)))
            if even + 1 <= last:
                given.append((exchange(got, 1), held(even + 1, 1, 4)))
        if far:
            given += [(got, held(steps, 1, 2)) for got, steps in zip(far_got, far)]
            handed = exchange(jnp.concatenate(far_got, axis=0), 1)
            given.append((handed, [place for steps in far for place in held(steps, 3, 2)]))
        octets = range(reach)
        if not far:
            return finish(given, list(octets), None, lead=True)
        first = [octet for octet in octets if octet >= far[0]]
        early = first, finish(given, first, None, lead=True)
        return finish(given, [octet for octet in octets if octet < far[0]], early, lead=True)

    gathered = lax.all_gather(white, "win", tiled=True)

    def whole(steps):
        return [(steps, group) for group in range(win_count)]

    given = [(gathered, whole(0))]
    for steps in range(reach + 1):
        pairs = [
            (device(c + reach * w + steps, w), device(c, w))
            for w in range(win_count)
            for c in range(chan_count)
            if c + reach * w + steps < chan_count
        ]
        if pairs:
            given.append((lax.ppermute(gathered, axes, pairs), whole(steps)))
    return finish(given, list(range(reach)), None, lead=False)


def solution(mesh):
    in_specs = (P("win", "chan", None), P("chan"), P("chan"))
    out_specs = P("win", "chan", None)
    return jax.shard_map(local, mesh=mesh, in_specs=in_specs, out_specs=out_specs, check_vma=False)
```

```python
import functools
import itertools
import math

import jax
import jax.numpy as jnp
import ml_dtypes
import numpy as np
from jax import lax
from jax.experimental import pallas as pl
from jax.experimental.pallas import tpu as pltpu
from jax.sharding import PartitionSpec as P

NF = 256
MAXOFF = 256
MAXLAG = 200
EPS = 1e-06
WHITEN_BINS = 64
LANES = 128
SUB = 8
TILES = 2 * NF // LANES
BF16 = jnp.bfloat16
F32 = jnp.float32
MIB = 1 << 20


def split(table):
    high = table.astype(ml_dtypes.bfloat16)
    low = (table - high.astype(np.float64)).astype(ml_dtypes.bfloat16)
    return high, low


def phase(product, length):
    return (product % length) * (2.0 * math.pi / length)


def forward_tables(samples, chunk):
    freq = np.arange(1, NF + 1, dtype=np.int64)
    inner = phase(np.arange(chunk, dtype=np.int64)[:, None] * freq[None, :], samples)
    outer = phase(np.arange(samples // chunk, dtype=np.int64)[:, None] * chunk * freq[None, :], samples)
    twiddle = np.concatenate([np.cos(outer), np.sin(outer)], axis=1).astype(np.float32)
    return split(np.concatenate([np.cos(inner), -np.sin(inner)], axis=1)) + (twiddle,)


def inverse_tables(samples, scale):
    freq = np.arange(1, NF + 1, dtype=np.int64)
    lags = np.arange(-MAXLAG, 2 * LANES - MAXLAG, dtype=np.int64)
    angles = phase(freq[:, None] * lags[None, :], samples)
    return split(scale * np.concatenate([np.cos(angles), -np.sin(angles)], axis=0))


def halves(value):
    high = value.astype(BF16)
    return high, (value - high.astype(F32)).astype(BF16)


def mm(a, b):
    return jnp.dot(a, b, preferred_element_type=F32)


def column(ref, count):
    rows = lax.broadcasted_iota(jnp.int32, (count, LANES), 0)
    value = jnp.zeros((count, LANES), jnp.int32)
    for index in range(count):
        value = jnp.where(rows == index, ref[index], value)
    return value


def whiten_kernel(alive_hbm, limit_hbm, strain_hbm, table_hbm, twiddle_hbm, white_ref, limit_out, *scratch):
    alive_ref, limit_ref, strain_ref, table_ref, twiddle_ref, sems = scratch
    wins, chans, samples = strain_ref.shape
    chunk = table_ref.shape[0] // 2
    copies = [
        pltpu.make_async_copy(source, target, sems.at[index])
        for index, (source, target) in enumerate(
            [
                (strain_hbm, strain_ref),
                (table_hbm, table_ref),
                (twiddle_hbm, twiddle_ref),
                (alive_hbm, alive_ref),
                (limit_hbm, limit_ref),
            ]
        )
    ]
    for copy in copies:
        copy.start()
    block_r = lax.broadcasted_iota(jnp.int32, (NF, NF), 0) // WHITEN_BINS
    block_c = lax.broadcasted_iota(jnp.int32, (NF, NF), 1) // WHITEN_BINS
    mean = jnp.where(block_r == block_c, 1.0 / WHITEN_BINS, 0.0).astype(BF16)
    rows = wins * chans
    copies[0].wait()
    strain = strain_ref[...].reshape(rows, samples)
    pieces = samples // chunk
    stacked = jnp.concatenate([strain[:, a * chunk : (a + 1) * chunk] for a in range(pieces)], axis=0)
    x_high, x_low = halves(stacked)
    for copy in copies[1:]:
        copy.wait()
    high = table_ref[:chunk, :]
    part = mm(x_high, high) + mm(x_high, table_ref[chunk:, :]) + mm(x_low, high)
    real = jnp.zeros((rows, NF), F32)
    imag = jnp.zeros((rows, NF), F32)
    for a in range(pieces):
        p_re = part[a * rows : (a + 1) * rows, :NF]
        p_im = part[a * rows : (a + 1) * rows, NF:]
        cos = twiddle_ref[a : a + 1, :NF]
        sin = twiddle_ref[a : a + 1, NF:]
        real = real + p_re * cos + p_im * sin
        imag = imag + p_im * cos - p_re * sin
    magnitude = jnp.sqrt(real * real + imag * imag)
    m_high, m_low = halves(magnitude)
    level = mm(m_high, mean) + mm(m_low, mean) + EPS
    live = column(alive_ref, chans).astype(F32)
    limit_out[...] = column(limit_ref, chans)
    for w in range(wins):
        keep = slice(w * chans, (w + 1) * chans)
        for tile in range(TILES):
            source = real if tile < TILES // 2 else imag
            lanes = slice(tile % (TILES // 2) * LANES, (tile % (TILES // 2) + 1) * LANES)
            white_ref[(tile * wins + w) * chans : (tile * wins + w + 1) * chans, :] = (
                source[keep, lanes] / level[keep, lanes] * live
            )


def whiten(strain, alive, offset_limit):
    wins, chans, samples = strain.shape
    chunk = min(256, samples)
    high, low, twiddle = forward_tables(samples, chunk)
    table = np.concatenate([high, low], axis=0)
    rows = wins * chans
    return pl.pallas_call(
        whiten_kernel,
        out_shape=(
            jax.ShapeDtypeStruct((TILES * rows, LANES), F32),
            jax.ShapeDtypeStruct((chans, LANES), jnp.int32),
        ),
        in_specs=[pl.BlockSpec(memory_space=pltpu.HBM)] * 5,
        out_specs=(pl.BlockSpec(memory_space=pltpu.VMEM),) * 2,
        scratch_shapes=[
            pltpu.SMEM((chans,), jnp.int32),
            pltpu.SMEM((chans,), jnp.int32),
            pltpu.VMEM(strain.shape, F32),
            pltpu.VMEM(table.shape, BF16),
            pltpu.VMEM(twiddle.shape, F32),
            pltpu.SemaphoreType.DMA((5,)),
        ],
        compiler_params=pltpu.CompilerParams(vmem_limit_bytes=32 * MIB),
        cost_estimate=pl.CostEstimate(flops=6 * rows * samples * 2 * NF, bytes_accessed=4 * rows * samples, transcendentals=0),
        name="whiten",
    )(*[pltpu.with_memory_space_constraint(jnp.asarray(x), pltpu.HBM) for x in (alive, offset_limit, strain, table, twiddle)])


CHUNK = 4


def runs(octets, most):
    found = []
    for index, octet in enumerate(octets):
        if found and found[-1][1] + found[-1][2] == octet and found[-1][2] < most:
            found[-1][2] += 1
        else:
            found.append([index, octet, 1])
    return found


def correlate_kernel(places, needed, octets, early, wins, chans, share, lead, *refs):
    count = len(places)
    limit_ref = refs[0]
    blocks = refs[1 : count + 1]
    high_ref, low_ref = refs[count + 1 : count + 3]
    rest = refs[count + 3 :]
    early_ref = rest[0] if early else None
    out_ref, partner, x_high, x_low, lagged, out_sem, early_sem = rest[1 if early else 0 :]
    groups = partner.shape[0]
    place = lax.axis_index("win")
    half = TILES // 2

    def rows_of(first, length):
        return pl.ds(first * SUB, length * SUB)

    def early_stores():
        return [
            pltpu.make_async_copy(early_ref.at[rows_of(at, length)], out_ref.at[rows_of(octet, length)], early_sem.at[at])
            for at, octet, length in runs(early, len(early))
        ]

    def store(at, octet, length):
        target = out_ref.at[rows_of(octet if early else at, length)]
        return pltpu.make_async_copy(lagged.at[rows_of(at, length)], target, out_sem.at[at])

    pieces = runs(octets, CHUNK)

    def gather():
        chan, chan_count = lax.axis_index("chan"), lax.axis_size("chan")
        empty = {(steps, group) for steps in needed for group in range(groups)}
        for index in range(0 if lead else 1, count):
            for part, (steps, group) in enumerate(places[index]):
                if steps not in needed:
                    continue
                value = blocks[index][part]
                if lead and steps > 0:
                    value = jnp.where(chan + steps < chan_count, value, 0.0)
                first = needed.index(steps) * chans
                for t in range(half):
                    re, im = value[t], value[t + half]
                    partner[group, 3 * t, :, first : first + chans, :] = re
                    partner[group, 3 * t + 1, :, first : first + chans, :] = re + im
                    partner[group, 3 * t + 2, :, first : first + chans, :] = re - im
                empty.remove((steps, group))
        for steps, group in sorted(empty):
            first = needed.index(steps) * chans
            partner[group, :, :, first : first + chans, :] = jnp.zeros((3 * half, wins, chans, LANES), F32)

    def cross(octet):
        first = needed.index(octet) * SUB
        sums = [[jnp.zeros((chans, LANES), F32) for _ in range(3 * half)] for _ in range(SUB)]
        for part, (_, group) in enumerate(places[0]):
            for w in range(wins):
                for t in range(half):
                    a_re, a_im = blocks[0][part, t, w], blocks[0][part, t + half, w]
                    mine = (a_re + a_im, a_re, a_im)
                    for j in range(SUB):
                        for k in range(3):
                            theirs = partner[group, 3 * t + k, w, pl.ds(first + j + 1, SUB), :]
                            sums[j][3 * t + k] = sums[j][3 * t + k] + mine[k] * theirs
        return [
            [s[3 * t] - s[3 * t + 2] for t in range(half)] + [s[3 * t] - s[3 * t + 1] for t in range(half)] for s in sums
        ]

    def all_lags(high, low):
        def product(rows):
            table_high, table_low = high_ref[rows, :], low_ref[rows, :]
            x_h, x_l = high[:, rows], low[:, rows]
            table = jnp.concatenate([table_high, table_low, table_high], axis=0)
            return mm(jnp.concatenate([x_h, x_h, x_l], axis=1), table)

        even, odd = product(slice(0, NF)), product(slice(NF, 2 * NF))
        ahead, behind = even + odd, even - odd
        lane = lax.broadcasted_iota(jnp.int32, (high.shape[0], LANES), 1)
        tiles = [ahead]
        for tile in range(2, pl.cdiv(2 * MAXLAG, LANES)):
            fold = 2 * MAXLAG - tile * LANES
            source = behind[:, :LANES]
            index = fold - lane
            if fold >= LANES:
                source = jnp.where(lane <= fold - LANES, behind[:, LANES:], source)
                index = jnp.where(lane <= fold - LANES, index - LANES, index)
            tiles.append(jnp.take_along_axis(source, jnp.clip(index, 0, LANES - 1), axis=1))
        return jnp.concatenate(tiles, axis=1)[:, : 2 * MAXLAG]

    def work():
        for copy in early_stores():
            copy.start()
        gather()
        limit = limit_ref[...]
        for at, octet, length in pieces:
            for k in range(length):
                sums = cross(octet + k)
                offset = place * share + (octet + k) * SUB
                for j in range(0, SUB, 2):
                    pair = [
                        jnp.concatenate([jnp.where(limit > offset + i, value, 0.0) for value in sums[i]], axis=1)
                        for i in (j, j + 1)
                    ]
                    high, low = halves(jnp.concatenate(pair, axis=0))
                    first = ((at + k) * SUB + j) * chans
                    x_high[first : first + 2 * chans, :] = high
                    x_low[first : first + 2 * chans, :] = low
            rows = slice(at * SUB * chans, (at + length) * SUB * chans)
            high, low = x_high[rows, :], x_low[rows, :]
            result = all_lags(high, low)
            lagged[at * SUB : (at + length) * SUB] = result.reshape(length * SUB, chans, result.shape[1])
            store(at, octet, length).start()
        for copy in early_stores() + [store(*piece) for piece in pieces]:
            copy.wait()

    def blank():
        lagged[...] = jnp.zeros(lagged.shape, F32)
        copies = early_stores() + [store(*piece) for piece in pieces]
        for copy in copies:
            copy.start()
        for copy in copies:
            copy.wait()

    if lead:
        pl.when(place == 0)(work)
        pl.when(place != 0)(blank)
    else:
        work()


def correlate(given, octets, early, limit, wins, chans, share, samples, scale, lead):
    high, low = inverse_tables(samples, scale)
    needed = sorted({octet + step for octet in octets for step in (0, 1)})
    used = [item for index, item in enumerate(given) if index == 0 or any(steps in needed for steps, _ in item[1])]
    groups = len(given[0][1])
    size = len(octets) * SUB
    rows = size * chans
    lags = 2 * MAXLAG
    early_octets, early_result = early if early else ((), None)
    places = [item[1] for item in used]
    body = functools.partial(correlate_kernel, places, needed, octets, early_octets, wins, chans, share, lead)
    done = early is not None or len(octets) * SUB == share
    return pl.pallas_call(
        body,
        out_shape=jax.ShapeDtypeStruct((size + len(early_octets) * SUB, chans, lags), F32),
        in_specs=[pl.BlockSpec(memory_space=pltpu.VMEM)] * (len(used) + 3)
        + [pl.BlockSpec(memory_space=pl.ANY)] * bool(early),
        out_specs=pl.BlockSpec(memory_space=pl.ANY),
        scratch_shapes=[
            pltpu.VMEM((groups, 3 * TILES // 2, wins, len(needed) * SUB, LANES), F32),
            pltpu.VMEM((rows, 2 * NF), BF16),
            pltpu.VMEM((rows, 2 * NF), BF16),
            pltpu.VMEM((size, chans, lags), F32),
            pltpu.SemaphoreType.DMA((len(octets),)),
            pltpu.SemaphoreType.DMA((max(1, len(early_octets)),)),
        ],
        compiler_params=pltpu.CompilerParams(vmem_limit_bytes=32 * MIB),
        cost_estimate=pl.CostEstimate(
            flops=6 * rows * 2 * NF * lags if done else 0,
            bytes_accessed=4 * rows * lags if done else 0,
            transcendentals=0,
        ),
        name="correlate",
    )(
        limit,
        *[block.reshape(-1, TILES, wins, chans, LANES) for block, _ in used],
        high,
        low,
        *([early_result] if early else []),
    )


def local(strain, offset_limit, alive):
    win_dev, ch_dev, samples = strain.shape
    win_count = lax.axis_size("win")
    chan_count = lax.axis_size("chan")
    scale = 1.0 / math.sqrt(NF * win_dev * win_count)
    share = MAXOFF // win_count
    reach = share // ch_dev
    axes = ("chan", "win")
    white, limit = whiten(strain, alive, offset_limit)
    finish = functools.partial(
        correlate,
        limit=limit,
        wins=win_dev,
        chans=ch_dev,
        share=share,
        samples=samples,
        scale=scale,
    )

    def device(chan, win):
        return chan * win_count + win

    def exchange(value, mask):
        pairs = [(device(c, w), device(c, w ^ mask)) for c in range(chan_count) for w in range(win_count)]
        return lax.ppermute(value, axes, pairs)

    def shift(wanted):
        sources = [w for w in range(win_count) if w not in [source for _, source in wanted.values()]]
        targets = [w for w in range(win_count) if w not in wanted]

        def cost(order):
            return sum(100 if s == t else (s ^ t) // 2 for s, t in zip(order, targets))

        idle = dict(zip(targets, min(itertools.permutations(sources), key=cost)))
        moves = {**wanted, **{target: (0, source) for target, source in idle.items()}}
        return [
            (device((c + steps) % chan_count, source), device(c, target))
            for target, (steps, source) in moves.items()
            for c in range(chan_count)
        ]

    if win_count == 4 and chan_count * ch_dev <= share:
        def held(steps, source, parts):
            return [(steps, source ^ part) for part in range(parts)]

        def join(value, mask):
            return jnp.concatenate([value, exchange(value, mask)], axis=0)

        chip = join(white, 1)
        far = [chan_count - 2, chan_count - 1] if chan_count >= 4 else []
        block = join(chip, 2)
        far_got = [lax.ppermute(chip, axes, shift({0: (steps, 1), 1: (steps, 3)})) for steps in reversed(far)][::-1]
        given = [(block, held(0, 0, 4))]
        last = chan_count - 1 - len(far)
        if chan_count > 1:
            given.append((lax.ppermute(block, axes, shift({0: (1, 1)})), held(1, 1, 4)))
        for even in range(2, last + 1, 2):
            wanted = {0: (even, 3)}
            if even + 1 <= last:
                wanted[1] = (even + 1, 1)
            got = lax.ppermute(block, axes, shift(wanted))
            given.append((got, held(even, 3, 4)))
            if even + 1 <= last:
                given.append((exchange(got, 1), held(even + 1, 1, 4)))
        if far:
            given += [(got, held(steps, 1, 2)) for got, steps in zip(far_got, far)]
            handed = exchange(jnp.concatenate(far_got, axis=0), 1)
            given.append((handed, [place for steps in far for place in held(steps, 3, 2)]))
        octets = range(reach)
        if not far:
            return finish(given, list(octets), None, lead=True)
        first = [octet for octet in octets if octet >= far[0]]
        early = first, finish(given, first, None, lead=True)
        return finish(given, [octet for octet in octets if octet < far[0]], early, lead=True)

    gathered = lax.all_gather(white, "win", tiled=True)

    def whole(steps):
        return [(steps, group) for group in range(win_count)]

    given = [(gathered, whole(0))]
    for steps in range(reach + 1):
        pairs = [
            (device(c + reach * w + steps, w), device(c, w))
            for w in range(win_count)
            for c in range(chan_count)
            if c + reach * w + steps < chan_count
        ]
        if pairs:
            given.append((lax.ppermute(gathered, axes, pairs), whole(steps)))
    return finish(given, list(range(reach)), None, lead=False)


def solution(mesh):
    in_specs = (P("win", "chan", None), P("chan"), P("chan"))
    out_specs = P("win", "chan", None)
    return jax.shard_map(local, mesh=mesh, in_specs=in_specs, out_specs=out_specs, check_vma=False)
```
